32 devices in a mesh: dp: 8 (over z, x), chan: 4 (over y, core).
Axes of the slice: x: 2, y: 2, z: 4, core: 2. Of those that a mesh axis runs over, the one named last changes fastest.
Arguments:
- inputs: bfloat16 [64, 128, 512], P(('dp', 'chan')), may hold values from -6 to 6
- cotangent: bfloat16 [64, 128, 512], P(('dp', 'chan')), may hold values from -6 to 6
- expand_w: bfloat16 [512, 2048], P(None, 'chan'), may hold values from -0.25 to 0.25
- expand_b: float32 [2048], P('chan'), may hold values from -3 to 3
- depth_k: float32 [25, 2048], P(None, 'chan'), may hold values from -1.25 to 1.25
- depth_b: float32 [2048], P('chan'), may hold values from -3 to 3
- project_w: bfloat16 [2048, 512], P('chan'), may hold values from -0.125 to 0.125
Outputs:
- input_grad: bfloat16 [64, 128, 512], P(('dp', 'chan'))
- expand_w_grad: float32 [512, 2048], P(None, 'chan')
- expand_b_grad: float32 [2048], P('chan')
- depth_k_grad: float32 [25, 2048], P(None, 'chan')
- depth_b_grad: float32 [2048], P('chan')
- project_w_grad: float32 [2048, 512], P('chan')
The draws below stay inside these ranges and needn't reach their ends.
All inputs are finite; a program needn't handle non-finite values.
Results may differ from the reference program's by a relative error of at most 0.007.
Values may be sent and summed in bfloat16 or wider, within the bound.
No kernel may reach another device: no remote copies, remote signals or barrier semaphores. Data moves between devices by JAX's collectives and lax.ppermute only.
A program may use at most 64 MiB of HBM per device.

```python
import jax
import jax.numpy as jnp
from jax import lax

C = 512
H = 2048
WIDTH = 128
ROWS = 64


def spiked(values, own_key, source, target, blocks, factor):
    def block_of(dim):
        return (jnp.arange(values.shape[dim]) // (values.shape[dim] // blocks)).reshape((-1,) + (1,) * (values.ndim - 1 - dim))

    first = jax.random.permutation(own_key, blocks)[block_of(target)]
    far = (block_of(target) + blocks // 2) % blocks
    return jnp.where((block_of(source) == first) | (block_of(source) == far), factor * values, values)


def shard_levels(own_key, dims, pieces, low, top_value):
    def one(axis_at, parts):
        draws = jax.random.uniform(jax.random.fold_in(jax.random.fold_in(own_key, 6), axis_at), (parts,), jnp.float32, low / len(pieces), top_value / len(pieces))
        return jnp.repeat(jnp.exp(draws), dims[axis_at] // parts).reshape((-1,) + (1,) * (len(dims) - axis_at - 1))

    gain = one(*pieces[0])
    for cut in pieces[1:]:
        gain = gain * one(*cut)
    return gain


def scatter_about(own_key, shape, width, limit, split=(), kind=jnp.bfloat16):
    loudness = shard_levels(own_key, shape, split, -0.22, 0.18) if split else 1.0
    drawn = jax.random.normal(own_key, shape, jnp.float32) * width * loudness
    return jnp.minimum(jnp.maximum(drawn, -limit), limit).astype(kind)


def gaussian_with(stream_key, shape, scale, reach, split, heavy, kind=jnp.bfloat16):
    values = scale * jax.random.normal(stream_key, shape, jnp.float32)
    if split:
        values = values * shard_levels(stream_key, shape, split, -0.22, 0.18)
    return jnp.clip(spiked(values, jax.random.fold_in(stream_key, 3), *heavy), -reach, reach).astype(kind)


def setup_inputs(seed: int = 0) -> dict:
    seeds = jax.random.split(jax.random.key(seed), 8)
    return {
        "inputs": scatter_about(seeds[0], (ROWS, WIDTH, C), 1.0, 6.0, ((0, 32),)),
        "cotangent": gaussian_with(seeds[1], (ROWS, WIDTH, C), 1.0, 6.0, ((0, 32),), (0, 2, 32, 2.75)),
        "expand_w": scatter_about(seeds[2], (C, H), C ** -0.5, 0.25, ((1, 4),)),
        "expand_b": scatter_about(seeds[3], (H,), 0.5, 3.0, ((0, 4),), jnp.float32),
        "depth_k": scatter_about(seeds[4], (25, H), 25 ** -0.5, 1.25, ((1, 4),), jnp.float32),
        "depth_b": scatter_about(seeds[5], (H,), 0.5, 3.0, ((0, 4),), jnp.float32),
        "project_w": scatter_about(seeds[6], (H, C), H ** -0.5, 0.125, ((0, 4),)),
    }


def gelu_parts(pre):
    cdf = 0.5 * (1.0 + lax.erf(pre * 0.7071067811865476))
    dens = jnp.exp(-0.5 * pre * pre) * 0.3989422804014327
    return pre * cdf, cdf + pre * dens


def reference(inputs, cotangent, expand_w, expand_b, depth_k, depth_b, project_w):
    blocks = 4
    hblk = H // blocks
    nrows = inputs.shape[0]
    ncols = inputs.shape[1]
    flat_inputs = inputs.reshape(nrows * ncols, C)
    flat_cotan = cotangent.reshape(nrows * ncols, C)
    stack_w1 = expand_w.reshape(C, blocks, hblk).transpose(1, 0, 2)
    stack_b1 = expand_b.reshape(blocks, hblk)
    stack_k = depth_k.reshape(25, blocks, hblk).transpose(1, 0, 2)
    stack_bd = depth_b.reshape(blocks, hblk)
    stack_w2 = project_w.reshape(blocks, hblk, C)

    def one_block(total, weights):
        w_one, b_one, kernel, b_two, w_two = weights
        pre_one = jnp.dot(flat_inputs, w_one, preferred_element_type=jnp.float32).reshape(nrows, ncols, hblk) + b_one
        hidden, slope_one = gelu_parts(pre_one)
        hidden = hidden.astype(jnp.bfloat16)
        padded = jnp.pad(hidden, ((2, 2), (2, 2), (0, 0))).astype(jnp.float32)
        pre_two = jnp.zeros((nrows, ncols, hblk), jnp.float32) + b_two
        for row_tap in range(5):
            for col_tap in range(5):
                pre_two = pre_two + kernel[5 * row_tap + col_tap] * padded[row_tap:row_tap + nrows, col_tap:col_tap + ncols]
        mixed, slope_two = gelu_parts(pre_two)
        mixed = mixed.astype(jnp.bfloat16).reshape(nrows * ncols, hblk)
        grad_w2 = jnp.dot(mixed.T, flat_cotan, preferred_element_type=jnp.float32)
        grad_mixed = jnp.dot(flat_cotan, w_two.T, preferred_element_type=jnp.float32).reshape(nrows, ncols, hblk)
        grad_pre = (grad_mixed * slope_two).astype(jnp.bfloat16)
        grad_pre_f = grad_pre.astype(jnp.float32)
        grad_bd = jnp.sum(grad_pre_f, axis=(0, 1))
        grad_pad = jnp.pad(grad_pre_f, ((2, 2), (2, 2), (0, 0)))
        taps = []
        grad_hidden = jnp.zeros((nrows, ncols, hblk), jnp.float32)
        for row_tap in range(5):
            for col_tap in range(5):
                taps.append(jnp.sum(padded[row_tap:row_tap + nrows, col_tap:col_tap + ncols] * grad_pre_f, axis=(0, 1)))
                grad_hidden = grad_hidden + kernel[5 * row_tap + col_tap] * grad_pad[4 - row_tap:4 - row_tap + nrows, 4 - col_tap:4 - col_tap + ncols]
        grad_k = jnp.stack(taps, axis=0)
        grad_act = (grad_hidden * slope_one).astype(jnp.bfloat16).reshape(nrows * ncols, hblk)
        grad_b1 = jnp.sum(grad_act.astype(jnp.float32), axis=0)
        grad_w1 = jnp.dot(flat_inputs.T, grad_act, preferred_element_type=jnp.float32)
        partial_value = jnp.dot(grad_act, w_one.T, preferred_element_type=jnp.float32)
        return total + partial_value, (grad_w1, grad_b1, grad_k, grad_bd, grad_w2)

    start_total = jnp.zeros((nrows * ncols, C), jnp.float32)
    total, grads = lax.scan(one_block, start_total, (stack_w1, stack_b1, stack_k, stack_bd, stack_w2))
    grad_w1, grad_b1, grad_k, grad_bd, grad_w2 = grads
    input_grad = (flat_cotan.astype(jnp.float32) + total).astype(jnp.bfloat16).reshape(nrows, ncols, C)
    return (input_grad,
            grad_w1.transpose(1, 0, 2).reshape(C, H),
            grad_b1.reshape(H),
            grad_k.transpose(1, 0, 2).reshape(25, H),
            grad_bd.reshape(H),
            grad_w2.reshape(H, C))
```

```python
import jax
import jax.numpy as jnp
from jax import lax
from jax.experimental import pallas as pl
from jax.experimental.pallas import tpu as pltpu
from jax.sharding import PartitionSpec as P

BF = jnp.bfloat16
F32 = jnp.float32
AXES = ("dp", "chan")
VMEM = pl.BlockSpec(memory_space=pltpu.VMEM)
SMEM = pl.BlockSpec(memory_space=pltpu.SMEM)
EDGE = 8


def params():
    return pltpu.CompilerParams(vmem_limit_bytes=48 * 1024 * 1024)


def cost(flops, nbytes, trans=0):
    return pl.CostEstimate(flops=flops, bytes_accessed=nbytes, transcendentals=trans)


def gelu_parts(pre):
    cdf = 0.5 * (1.0 + lax.erf(pre * 0.7071067811865476))
    dens = jnp.exp(-0.5 * pre * pre) * 0.3989422804014327
    return pre * cdf, cdf + pre * dens


def hop(value, dp_xor, chan_xor):
    ndp, nchan = lax.axis_size("dp"), lax.axis_size("chan")
    pairs = [
        (d * nchan + c, (d ^ dp_xor) * nchan + (c ^ chan_xor))
        for d in range(ndp)
        for c in range(nchan)
    ]
    return lax.ppermute(value, AXES, pairs)


def shift(value, step):
    ndp, nchan = lax.axis_size("dp"), lax.axis_size("chan")
    pairs = [
        (d * nchan + c, (d + step) * nchan + c)
        for d in range(ndp)
        if 0 <= d + step < ndp
        for c in range(nchan)
    ]
    return lax.ppermute(value, AXES, pairs)


def gathered(block):
    across, beside, corner = hop(block, 1, 0), hop(block, 0, 2), hop(block, 1, 2)
    near = {0: block, 2: beside, 4: across, 6: corner}
    return [near[k] if k in near else hop(near[k - 1], 0, 1) for k in range(8)]


def scattered(chunks, zpos, groups):
    own = lax.dynamic_index_in_dim(chunks, zpos, 0, keepdims=False).astype(F32)
    for k in range(1, groups):
        part = lax.dynamic_index_in_dim(chunks, zpos ^ k, 0, keepdims=False)
        own = own + hop(part.astype(BF), 2 * k, 0).astype(F32)
    return own.astype(BF)


def spread(chunk, groups):
    return [[hop(chunk, 2 * k + m, 0) if k + m else chunk for m in range(2)] for k in range(groups)]


def expand_kernel(me, *refs):
    pieces, (w, b, hid, slope, rows, pre) = refs[:8], refs[8:]
    n, ncols, cin = pieces[0].shape
    step = 64
    for k, piece in enumerate(pieces):
        at = (me[0] ^ k) * n
        rows[pl.ds(at, n)] = piece[...]
        pre[...] = jnp.dot(piece[...].reshape(n * ncols, cin), w[...], preferred_element_type=F32) + b[...]
        for r in range(n):

            def body(i, carry, r=r, at=at):
                src = pl.ds(pl.multiple_of(r * ncols + i * step, step), step)
                dst = pl.ds(pl.multiple_of(i * step, step), step)
                h, s = gelu_parts(pre[src, :])
                hid[at + r, dst, :] = h.astype(BF)
                slope[at + r, dst, :] = s.astype(BF)
                return carry

            lax.fori_loop(0, ncols // step, body, 0)


def project_kernel(me, *refs):
    pieces, (w, out, rows) = refs[:8], refs[8:]
    n, ncols, cin = pieces[0].shape
    for k, piece in enumerate(pieces):
        at = (me[0] ^ k) * n
        rows[pl.ds(at, n)] = piece[...]
        res = lax.dot_general(
            piece[...].reshape(n * ncols, cin), w[...], (((1,), (1,)), ((), ())), preferred_element_type=F32
        )
        out[pl.ds(at, n)] = res.reshape(n, ncols, -1)


def load_padded(pad, top, mid, bottom):
    nrows, ncols, lanes = mid.shape
    zeros = jnp.zeros((nrows + 4, EDGE, lanes), F32)
    pad[:, 0:EDGE, :] = zeros
    pad[:, EDGE + ncols :, :] = zeros
    pad[0:2, EDGE : EDGE + ncols, :] = top[...].astype(F32)
    pad[nrows + 2 :, EDGE : EDGE + ncols, :] = bottom[...].astype(F32)

    def body(r, carry):
        pad[r + 2, EDGE : EDGE + ncols, :] = mid[r].astype(F32)
        return carry

    lax.fori_loop(0, nrows, body, 0)


def conv_tiles(pad, taps, nrows, ncols, flip, emit):
    cols = 16

    def body(i, carry):
        w0 = i * cols
        for r0 in range(0, nrows, 4):
            acc = [None] * 4
            for j in range(5):
                xs = [pad[r0 + q, pl.ds(w0 + (EDGE - 2) + j, cols), :] for q in range(8)]
                for q in range(5):
                    t = 5 * q + j
                    tap = taps[(24 - t if flip else t) : (25 - t if flip else t + 1), :]
                    for r in range(4):
                        term = tap * xs[r + q]
                        acc[r] = term if acc[r] is None else acc[r] + term
            emit(r0, pl.ds(pl.multiple_of(w0, cols), cols), acc)
        return carry

    lax.fori_loop(0, ncols // cols, body, 0)


def middle_kernel(top, mid, bottom, gm, taps, bias, mixed, gp, pad):
    nrows, ncols, _ = mid.shape
    load_padded(pad, top, mid, bottom)

    def emit(r0, w, acc):
        for r in range(4):
            m, s = gelu_parts(acc[r] + bias[...])
            mixed[r0 + r, w, :] = m.astype(BF)
            gp[r0 + r, w, :] = (gm[r0 + r, w, :] * s).astype(BF)

    conv_tiles(pad, taps, nrows, ncols, False, emit)


def taps_kernel(top, mid, bottom, gp, grad_k, grad_b, pad, gpf):
    nrows, ncols, lanes = mid.shape
    load_padded(pad, top, mid, bottom)

    def widen(r, carry):
        gpf[r] = gp[r].astype(F32)
        return carry

    lax.fori_loop(0, nrows, widen, 0)

    def body(i, accs):
        accs = list(accs)
        w0 = i * 8
        for j in range(5):
            xs = [pad[q, pl.ds(w0 + (EDGE - 2) + j, 8), :] for q in range(4)]
            for r in range(nrows):
                xs.append(pad[r + 4, pl.ds(w0 + (EDGE - 2) + j, 8), :])
                g = gpf[r, pl.ds(pl.multiple_of(w0, 8), 8), :]
                for q in range(5):
                    accs[5 * q + j] = accs[5 * q + j] + xs[r + q] * g
                if j == 0:
                    accs[25] = accs[25] + g
        return tuple(accs)

    accs = lax.fori_loop(0, ncols // 8, body, tuple(jnp.zeros((8, lanes), F32) for _ in range(26)))
    for t in range(25):
        grad_k[t : t + 1, :] = jnp.sum(accs[t], axis=0, keepdims=True)
    grad_b[...] = jnp.sum(accs[25], axis=0, keepdims=True)


def back_kernel(top, mid, bottom, slope, taps, act, grad_b, pad, total):
    nrows, ncols, lanes = mid.shape
    load_padded(pad, top, mid, bottom)
    total[...] = jnp.zeros_like(total)

    def emit(r0, w, acc):
        part = jnp.zeros((8, lanes), F32)
        for r in range(4):
            a = (acc[r] * slope[r0 + r, w, :].astype(F32)).astype(BF)
            act[r0 + r, w, :] = a
            part = part + jnp.sum(a.astype(F32).reshape(-1, 8, lanes), axis=0)
        total[...] += part

    conv_tiles(pad, taps, nrows, ncols, True, emit)
    grad_b[...] = jnp.sum(total[...], axis=0, keepdims=True)


def place_kernel(where, *refs):
    blocks, out = refs[:-1], refs[-1]
    n, lanes = blocks[0].shape
    for k, block in enumerate(blocks):
        r, c = where[2 * k], where[2 * k + 1]
        out[pl.ds(pl.multiple_of(r * n, n), n), pl.ds(pl.multiple_of(c * lanes, lanes), lanes)] = block[...].astype(F32)


def shards(inputs, cotangent, expand_w, expand_b, depth_k, depth_b, project_w):
    chan = lax.axis_index("chan")
    pair = lax.rem(lax.axis_index("dp"), 2)
    zpos = lax.div(lax.axis_index("dp"), 2)
    groups = lax.axis_size("dp") // 2
    own_rows, ncols, cin = inputs.shape
    nrows = 8 * own_rows
    hslice = expand_w.shape[1]
    half = hslice // 2
    lanes = 128
    npix = nrows * ncols
    me = (pair * 4 + chan).astype(jnp.int32).reshape(1)

    w1 = lax.dynamic_slice_in_dim(expand_w, pair * half, half, axis=1)
    w2 = lax.dynamic_slice_in_dim(project_w, pair * half, half, axis=0)
    b1 = lax.dynamic_slice_in_dim(expand_b, pair * half, half).reshape(1, half)
    bd = lax.dynamic_slice_in_dim(depth_b, pair * half, half).reshape(1, half)
    taps = lax.dynamic_slice_in_dim(depth_k, pair * half, half, axis=1)

    def array(*shape, dtype=BF):
        return jax.ShapeDtypeStruct(shape, dtype)

    full = array(nrows, ncols, half)
    in_pieces = gathered(inputs)
    hidden, slope_one, rows_in = pl.pallas_call(
        expand_kernel,
        out_shape=(full, full, array(nrows, ncols, cin)),
        in_specs=[SMEM] + [VMEM] * 10,
        out_specs=(VMEM,) * 3,
        scratch_shapes=[pltpu.VMEM((own_rows * ncols, half), F32)],
        compiler_params=params(),
        cost_estimate=cost(2 * npix * cin * half, 4 * npix * cin),
        name="expand",
    )(me, *in_pieces, w1, b1)

    hid_top = shift(hidden[nrows - 2 :], 2)
    hid_bottom = shift(hidden[:2], -2)
    cot_pieces = gathered(cotangent)
    grad_mixed, rows_cot = pl.pallas_call(
        project_kernel,
        out_shape=(array(nrows, ncols, half, dtype=F32), array(nrows, ncols, cin)),
        in_specs=[SMEM] + [VMEM] * 9,
        out_specs=(VMEM,) * 2,
        compiler_params=params(),
        cost_estimate=cost(2 * npix * cin * half, 4 * npix * cin),
        name="project",
    )(me, *cot_pieces, w2)

    def rows_spec(n):
        return pl.BlockSpec((n, ncols, lanes), lambda i: (0, 0, i))

    def flat_spec(n):
        return pl.BlockSpec((n, lanes), lambda i: (0, i))

    grid = (half // lanes,)
    padded = pltpu.VMEM((nrows + 4, ncols + 2 * EDGE, lanes), F32)
    halo_specs = [rows_spec(2), rows_spec(nrows), rows_spec(2)]
    vpu = cost(100 * npix * half, 8 * npix * half)
    mixed, grad_pre = pl.pallas_call(
        middle_kernel,
        grid=grid,
        out_shape=(full, full),
        in_specs=halo_specs + [rows_spec(nrows), flat_spec(25), flat_spec(1)],
        out_specs=(rows_spec(nrows),) * 2,
        scratch_shapes=[padded],
        compiler_params=params(),
        cost_estimate=vpu,
        name="middle",
    )(hid_top, hidden, hid_bottom, grad_mixed, taps, bd)

    gp_top = shift(grad_pre[nrows - 2 :], 2)
    gp_bottom = shift(grad_pre[:2], -2)
    flat_cot = rows_cot.reshape(npix, cin)
    grad_w2 = jnp.dot(mixed.reshape(npix, half).T, flat_cot, preferred_element_type=F32)
    w2_own = scattered(grad_w2.reshape(groups, half // groups, cin), zpos, groups)

    grad_k, grad_bd = pl.pallas_call(
        taps_kernel,
        grid=grid,
        out_shape=(array(25, half, dtype=F32), array(1, half, dtype=F32)),
        in_specs=halo_specs + [rows_spec(nrows)],
        out_specs=(flat_spec(25), flat_spec(1)),
        scratch_shapes=[padded, pltpu.VMEM((nrows, ncols, lanes), F32)],
        compiler_params=params(),
        cost_estimate=vpu,
        name="taps",
    )(hid_top, hidden, hid_bottom, grad_pre)

    grad_act, grad_b1 = pl.pallas_call(
        back_kernel,
        grid=grid,
        out_shape=(full, array(1, half, dtype=F32)),
        in_specs=halo_specs + [rows_spec(nrows), flat_spec(25)],
        out_specs=(rows_spec(nrows), flat_spec(1)),
        scratch_shapes=[padded, pltpu.VMEM((8, lanes), F32)],
        compiler_params=params(),
        cost_estimate=vpu,
        name="back",
    )(gp_top, grad_pre, gp_bottom, slope_one, taps)

    core = lax.rem(chan, 2)
    by_core = grad_act.reshape(4, 2, own_rows * ncols, half)

    def share(which):
        act = lax.dynamic_index_in_dim(by_core, which, 1, keepdims=False)
        return jnp.einsum("pth,ch->ptc", act, w1, preferred_element_type=F32)

    other = hop(share(1 - core).astype(BF), 0, 1)
    flat_act = grad_act.reshape(npix, half)
    grad_w1 = jnp.dot(rows_in.reshape(npix, cin).T, flat_act, preferred_element_type=F32)
    tail_rows = 16 * groups
    small = jnp.concatenate([grad_k, grad_bd, grad_b1, jnp.zeros((tail_rows - 27, half), F32)], axis=0)
    w1_chunks = jnp.concatenate(
        [grad_w1.reshape(groups, cin // groups, half), small.reshape(groups, 16, half)], axis=1
    )
    chip_sum = share(core) + other.astype(F32)
    chip = pair * 2 + lax.div(chan, 2)

    def chip_part(k):
        return lax.dynamic_index_in_dim(chip_sum, chip ^ k, 0, keepdims=False)

    own_part = chip_part(0)
    for k, (a, b) in ((1, (0, 2)), (2, (1, 0)), (3, (1, 2))):
        own_part = own_part + hop(chip_part(k).astype(BF), a, b).astype(F32)
    input_grad = (cotangent.astype(F32) + own_part.reshape(cotangent.shape)).astype(BF)

    w1_own = scattered(w1_chunks, zpos, groups)

    def placed(blocks, where, shape):
        return pl.pallas_call(
            place_kernel,
            out_shape=jax.ShapeDtypeStruct(shape, F32),
            in_specs=[SMEM] + [VMEM] * len(blocks),
            out_specs=VMEM,
            compiler_params=params(),
            name="place",
        )(jnp.stack(where).astype(jnp.int32), *blocks)

    w2_blocks, w2_where, w1_blocks, small_blocks, w1_where = [], [], [], [], []
    w2_all, w1_all = spread(w2_own, groups), spread(w1_own, groups)
    for k in range(groups):
        for m in range(2):
            w2_blocks.append(w2_all[k][m])
            w2_where += [(pair ^ m) * groups + (zpos ^ k), 0 * zpos]
            w1_blocks.append(w1_all[k][m][: cin // groups])
            small_blocks.append(w1_all[k][m][cin // groups :])
            w1_where += [zpos ^ k, pair ^ m]
    out_w2 = placed(w2_blocks, w2_where, (hslice, cin))
    out_w1 = placed(w1_blocks, w1_where, (cin, hslice))
    out_small = placed(small_blocks, w1_where, (tail_rows, hslice))
    return (input_grad, out_w1, out_small[26], out_small[:25], out_small[25], out_w2)


def solution(mesh):
    in_specs = (
        P(("dp", "chan"), None, None),
        P(("dp", "chan"), None, None),
        P(None, "chan"),
        P("chan"),
        P(None, "chan"),
        P("chan"),
        P("chan", None),
    )
    out_specs = (
        P(("dp", "chan"), None, None),
        P(None, "chan"),
        P("chan"),
        P(None, "chan"),
        P("chan"),
        P("chan", None),
    )
    return jax.shard_map(shards, mesh=mesh, in_specs=in_specs, out_specs=out_specs, check_vma=False)
```

```python
import jax
import jax.numpy as jnp
from jax import lax
from jax.experimental import pallas as pl
from jax.experimental.pallas import tpu as pltpu
from jax.sharding import PartitionSpec as P

BF = jnp.bfloat16
F32 = jnp.float32
AXES = ("dp", "chan")
VMEM = pl.BlockSpec(memory_space=pltpu.VMEM)
SMEM = pl.BlockSpec(memory_space=pltpu.SMEM)
ANY = pl.BlockSpec(memory_space=pl.ANY)
EDGE = 8
LANES = 128


def array(*shape, dtype=BF):
    return jax.ShapeDtypeStruct(shape, dtype)


def kernel(body, name, out, args, scratch=(), flops=0, nbytes=0, after=(), into=()):
    first, last = len(args), len(args) + len(after) + len(into)

    def run(*refs):
        body(*refs[:first], *refs[last:])

    return pl.pallas_call(
        run,
        out_shape=out,
        in_specs=[SMEM] + [VMEM] * (len(args) - 1) + [ANY] * len(after) + [VMEM] * len(into),
        out_specs=jax.tree.map(lambda _: VMEM, out),
        scratch_shapes=list(scratch),
        compiler_params=pltpu.CompilerParams(vmem_limit_bytes=16 * 1024 * 1024),
        cost_estimate=pl.CostEstimate(flops=flops, bytes_accessed=nbytes, transcendentals=0),
        input_output_aliases={len(args) + len(after) + i: i for i in range(len(into))},
        name=name,
    )(*args, *after, *into)


def gelu_parts(pre):
    cdf = 0.5 * (1.0 + lax.erf(pre * 0.7071067811865476))
    dens = jnp.exp(-0.5 * pre * pre) * 0.3989422804014327
    return pre * cdf, cdf + pre * dens


def hop(value, dp_xor, chan_xor):
    ndp, nchan = lax.axis_size("dp"), lax.axis_size("chan")
    pairs = [
        (d * nchan + c, (d ^ dp_xor) * nchan + (c ^ chan_xor))
        for d in range(ndp)
        for c in range(nchan)
    ]
    return lax.ppermute(value, AXES, pairs)


def cross(value, turn):
    ndp, nchan = lax.axis_size("dp"), lax.axis_size("chan")
    pairs = []
    for d in range(ndp):
        for c in range(nchan):
            to = (d ^ 1, c) if (c & 1) == turn else (d, c ^ 2)
            pairs.append((d * nchan + c, to[0] * nchan + to[1]))
    return lax.ppermute(value, AXES, pairs)


def meet(value, odd):
    ndp, nchan = lax.axis_size("dp"), lax.axis_size("chan")
    pairs = []
    for d in range(ndp):
        to = d + 2 if (d // 2) % 2 == odd else d - 2
        if 0 <= to < ndp:
            pairs += [(d * nchan + c, to * nchan + c) for c in range(nchan)]
    return lax.ppermute(value, AXES, pairs)


def tied(value, *others):
    return lax.optimization_barrier((value, *others))[0]


def prepare_kernel(pos, w1, b1, taps, b2, w2, rows, cot, w1_own, b1_own, taps_own, b2_own, w2_own, rows_own, cot_own):
    half = b1_own.shape[1]
    cut = pl.ds(pl.multiple_of(pos[1] * half, half), half)
    w1_own[...] = w1[:, cut]
    b1_own[...] = b1[:, cut]
    taps_own[...] = taps[:, cut]
    b2_own[...] = b2[:, cut]
    w2_own[...] = w2[cut, :]
    rows_own[...] = rows[...]
    cot_own[...] = cot[...]


def put_edges(pos, rows, edges):
    last = rows.shape[0] - 2
    odd = pos[2] & 1
    edges[0][...] = rows[pl.ds(last * (1 - odd), 2)]
    edges[1][...] = rows[pl.ds(last * odd, 2)]


def expand_kernel(order, pos, w, b, *refs):
    pieces, (hid, slope, *edges, pre) = refs[: len(order)], refs[len(order) :]
    n, ncols, cin = pieces[0].shape
    half = hid.shape[2]
    for k, piece in zip(order, pieces):
        at = (pos[0] ^ k) * n
        pre[...] = (
            jnp.dot(piece[...].reshape(n * ncols, cin), w[...], preferred_element_type=F32) + b[...]
        ).reshape(n, ncols, half)

        def body(r, carry, at=at):
            h, s = gelu_parts(pre[r])
            hid[at + r] = h.astype(BF)
            slope[at + r] = s.astype(BF)
            return carry

        lax.fori_loop(0, n, body, 0)
    if edges:
        put_edges(pos, hid, edges)


def load_padded(pos, pad, cut, mid, near=None, far=None, rows=None):
    nrows, ncols, _ = mid.shape
    zeros = jnp.zeros((nrows + 4, EDGE, LANES), F32)
    pad[:, 0:EDGE, :] = zeros
    pad[:, EDGE + ncols :, :] = zeros
    if near is not None:
        a, b = near[:, :, cut].astype(F32), far[:, :, cut].astype(F32)
        odd = (pos[2] & 1) == 1
        pad[0:2, EDGE : EDGE + ncols, :] = jnp.where(odd, a, b)
        pad[nrows + 2 :, EDGE : EDGE + ncols, :] = jnp.where(odd, b, a)

    def body(r, carry):
        pad[r + 2, EDGE : EDGE + ncols, :] = mid[r, :, cut].astype(F32)
        return carry

    for lo, hi in rows or ((0, nrows),):
        lax.fori_loop(lo, hi, body, 0)


def conv_tiles(pad, taps, cut, ncols, starts, nr, cols, flip, emit):
    def body(i, carry):
        w0 = i * cols
        for r0 in starts:
            acc = [None] * nr
            for j in range(5):
                xs = [pad[r0 + q, pl.ds(w0 + (EDGE - 2) + j, cols), :] for q in range(nr + 4)]
                for q in range(5):
                    t = 5 * q + j
                    t = 24 - t if flip else t
                    for r in range(nr):
                        term = taps[t : t + 1, cut] * xs[r + q]
                        acc[r] = term if acc[r] is None else acc[r] + term
            emit(r0, pl.ds(pl.multiple_of(w0, cols), cols), acc)
        return carry

    lax.fori_loop(0, ncols // cols, body, 0)


def cuts(half):
    return [slice(c, c + LANES) for c in range(0, half, LANES)]


def middle_kernel(inner, pos, taps, bias, *refs):
    (mid, mixed, slope, pad) = refs if inner else (refs[0], *refs[3:])
    near, far = (None, None) if inner else refs[1:3]
    nrows, ncols, half = mid.shape
    for cut in cuts(half):
        load_padded(pos, pad, cut, mid, near, far, None if inner else ((0, 4), (nrows - 4, nrows)))
        add = bias[:, cut]

        def emit(r0, w, acc, cut=cut, add=add):
            for r in range(len(acc)):
                m, s = gelu_parts(acc[r] + add)
                mixed[r0 + r, w, cut] = m.astype(BF)
                slope[r0 + r, w, cut] = s

        if inner:
            conv_tiles(pad, taps, cut, ncols, range(2, nrows - 2, 4), 4, 16, False, emit)
        else:
            conv_tiles(pad, taps, cut, ncols, (0, nrows - 2), 2, 32, False, emit)


def project_kernel(order, pos, weights, slope, *refs):
    pieces, (gp, *edges) = refs[: len(order)], refs[len(order) :]
    n, ncols, cin = pieces[0].shape
    half = gp.shape[2]
    for k, piece in zip(order, pieces):
        at = (pos[0] ^ k) * n
        res = lax.dot_general(
            piece[...].reshape(n * ncols, cin), weights[...], (((1,), (1,)), ((), ())), preferred_element_type=F32
        )
        gp[pl.ds(at, n)] = (res.reshape(n, ncols, half) * slope[pl.ds(at, n)]).astype(BF)
    if edges:
        put_edges(pos, gp, edges)


def outer_sum(pos, total, pieces, values, swap):
    n, ncols, _ = pieces[0].shape
    for k, piece in enumerate(pieces):
        a = piece[...].reshape(n * ncols, -1)
        b = values[pl.ds((pos[0] ^ k) * n, n)].reshape(n * ncols, -1)
        if swap:
            a, b = b, a
        part = lax.dot_general(a, b, (((0,), (0,)), ((), ())), preferred_element_type=F32)
        if k == 0:
            total[0 : part.shape[0], :] = part
        else:
            total[0 : part.shape[0], :] += part


def w2_kernel(pos, mixed, *refs):
    pieces, outs, total = refs[:8], refs[8:-1], refs[-1]
    outer_sum(pos, total, pieces, mixed, True)
    n = outs[0].shape[0]
    for k, ref in enumerate(outs):
        ref[...] = total[pl.ds(pl.multiple_of((pos[2] ^ k) * n, n), n), :].astype(ref.dtype)


def taps_kernel(pos, mid, near, far, gp, small, pad, gpf):
    nrows, ncols, half = mid.shape
    small[...] = jnp.zeros_like(small)
    for cut in cuts(half):
        load_padded(pos, pad, cut, mid, near, far)

        def widen(r, carry, cut=cut):
            gpf[r] = gp[r, :, cut].astype(F32)
            return carry

        lax.fori_loop(0, nrows, widen, 0)

        def body(i, accs):
            accs = list(accs)
            w0 = i * 8
            for j in range(5):
                xs = [pad[q, pl.ds(w0 + (EDGE - 2) + j, 8), :] for q in range(4)]
                for r in range(nrows):
                    xs.append(pad[r + 4, pl.ds(w0 + (EDGE - 2) + j, 8), :])
                    g = gpf[r, pl.ds(pl.multiple_of(w0, 8), 8), :]
                    for q in range(5):
                        accs[5 * q + j] = accs[5 * q + j] + xs[r + q] * g
                    if j == 0:
                        accs[25] = accs[25] + g
            return tuple(accs)

        zero = jnp.zeros((8, LANES), F32)
        accs = lax.fori_loop(0, ncols // 8, body, (zero,) * 26)
        for t in range(26):
            small[t : t + 1, cut] = jnp.sum(accs[t], axis=0, keepdims=True)


def back_kernel(pos, taps, mid, near, far, slope, act, grad_b, pad, total):
    nrows, ncols, half = mid.shape
    for cut in cuts(half):
        load_padded(pos, pad, cut, mid, near, far)
        total[...] = jnp.zeros_like(total)

        def emit(r0, w, acc, cut=cut):
            part = jnp.zeros((8, LANES), F32)
            for r in range(4):
                a = (acc[r] * slope[r0 + r, w, cut].astype(F32)).astype(BF)
                act[r0 + r, w, cut] = a
                part = part + jnp.sum(a.astype(F32).reshape(-1, 8, LANES), axis=0)
            total[...] += part

        conv_tiles(pad, taps, cut, ncols, range(0, nrows, 4), 4, 16, True, emit)
        grad_b[:, cut] = jnp.sum(total[...], axis=0, keepdims=True)


def w1_kernel(pos, act, small, grad_b, *refs):
    pieces, outs, total = refs[:8], refs[8:-1], refs[-1]
    outer_sum(pos, total, pieces, act, False)
    cin = pieces[0].shape[2]
    total[cin:, :] = small[...]
    total[cin + 26 : cin + 27, :] = grad_b[...]
    chunks = len(outs)
    n, m = cin // chunks, small.shape[0] // chunks
    for k, ref in enumerate(outs):
        at = pos[2] ^ k
        ref[0:n, :] = total[pl.ds(pl.multiple_of(at * n, n), n), :].astype(ref.dtype)
        ref[n:, :] = total[pl.ds(pl.multiple_of(cin + at * m, m), m), :].astype(ref.dtype)


def share(pos, act, w, chip_xor, core):
    ncols, half = act.shape[1:]
    n = act.shape[0] // 8
    at = (((pos[0] // 2) ^ chip_xor) * 2 + core) * n
    return lax.dot_general(
        act[pl.ds(at, n)].reshape(n * ncols, half), w[...], (((1,), (1,)), ((), ())), preferred_element_type=F32
    ).reshape(n, ncols, -1)


def core_kernel(pos, act, w, out):
    for k in range(4):
        out[k] = share(pos, act, w, k, 1 - pos[3]).astype(BF)


def chip_send_kernel(pos, act, w, other, out):
    for i, k in enumerate((2 - pos[3], 3)):
        out[i] = (share(pos, act, w, k, pos[3]) + other[k].astype(F32)).astype(BF)


def chip_keep_kernel(pos, act, w, other, out):
    for i, k in enumerate((0, 1 + pos[3])):
        out[i] = share(pos, act, w, k, pos[3]) + other[k].astype(F32)


def forward_kernel(pos, kept, arrived, out):
    out[...] = (kept[1] + arrived[1].astype(F32)).astype(BF)


def finish_kernel(pos, cot, kept, arrived, last, out):
    out[...] = (cot[...].astype(F32) + (kept[0] + arrived[0].astype(F32) + last[...].astype(F32))).astype(BF)


def column_kernel(pos, *refs):
    blocks, out = refs[:-1], refs[-1]
    for k, block in enumerate(blocks):
        out[pos[2] ^ k] = block[...]


def w2_place_kernel(pos, blocks, out):
    some, _, n, _ = blocks[0].shape
    groups = some * len(blocks)
    for b, block in enumerate(blocks):
        for a in range(some):
            for x in range(2):
                at = (pos[1] ^ x) * groups + (pos[2] ^ (len(blocks) * a + b))
                out[pl.ds(pl.multiple_of(at * n, n), n), :] = block[a, x].astype(F32)


def w1_place_kernel(pos, mine, other, out, grad_k, grad_bd, grad_b1, small):
    g, rows, half = mine.shape
    n = out.shape[0] // g
    m = rows - n
    for k, col in enumerate((mine, other)):
        cut = pl.ds(pl.multiple_of((pos[1] ^ k) * half, half), half)
        for i in range(g):
            out[i * n : (i + 1) * n, cut] = col[i, 0:n, :].astype(F32)
            small[i * m : (i + 1) * m, cut] = col[i, n:, :].astype(F32)
    grad_k[...] = small[0:25, :]
    grad_bd[...] = small[25:26, :]
    grad_b1[...] = small[26:27, :]


def last_kernel(pos, cot, kept, arrived, last, mine, other, *refs):
    blocks, (out, out_w2, out_w1, grad_k, grad_bd, grad_b1, small) = refs[:-7], refs[-7:]
    finish_kernel(pos, cot, kept, arrived, last, out)
    w2_place_kernel(pos, blocks, out_w2)
    w1_place_kernel(pos, mine, other, out_w1, grad_k, grad_bd, grad_b1, small)


def summed(own, sends):
    for k, send in enumerate(sends):
        own = own + hop(send, 2 * (k + 1), 0).astype(F32)
    return own.astype(BF)


def halved(chunks):
    arrived = hop(jnp.stack([chunks[1], chunks[3]]), 2, 0).astype(F32)
    return chunks[0] + arrived[0], chunks[2] + arrived[1]


def column(pos, chunk, groups, after=()):
    blocks = [hop(chunk, 2 * k, 0) if k else chunk for k in range(groups)]
    return kernel(column_kernel, "column", array(groups, *chunk.shape), (pos, *blocks), after=after)


def shards(inputs, cotangent, expand_w, expand_b, depth_k, depth_b, project_w):
    chan, dp = lax.axis_index("chan"), lax.axis_index("dp")
    pair, zpos = dp & 1, dp >> 1
    groups = lax.axis_size("dp") // 2
    own_rows, ncols, cin = inputs.shape
    nrows = 8 * own_rows
    hslice = expand_w.shape[1]
    half = hslice // 2
    npix = nrows * ncols
    pos = jnp.stack([pair * 4 + chan, pair, zpos, chan & 1]).astype(jnp.int32)

    full = array(nrows, ncols, half)
    mm = vpu = dict(flops=1024, nbytes=1024)
    pad = pltpu.VMEM((nrows + 4, ncols + 2 * EDGE, LANES), F32)

    mine = array(*inputs.shape)
    w1, b1, taps, bd, w2, rows_own, cot_own = kernel(
        prepare_kernel, "prepare",
        (array(cin, half), array(1, half, dtype=F32), array(25, half, dtype=F32), array(1, half, dtype=F32),
         array(half, cin), mine, mine),
        (pos, expand_w, expand_b.reshape(1, hslice), depth_k, depth_b.reshape(1, hslice), project_w, inputs, cotangent),
    )

    def expand(order, into=(), after=(), edges=()):
        return kernel(
            lambda *refs: expand_kernel(order, *refs), "expand%d" % order[0], (full, full) + edges,
            (pos, w1, b1, *(in_pieces[k] for k in order)), [pltpu.VMEM((own_rows, ncols, half), F32)],
            into=into, after=after, **mm,
        )

    in_pieces = {0: rows_own, 1: hop(inputs, 0, 1)}
    cot_pieces = {0: cot_own, 1: hop(cotangent, 0, 1)}
    steps = {4: (1, 0), 2: (0, 2), 6: (1, 2)}
    for k, step in steps.items():
        in_pieces[k] = hop(inputs, *step)
    first = expand((0, 1), after=(cot_pieces[1],))
    for k in steps:
        in_pieces[k + 1] = hop(tied(in_pieces[k], first[0]), 0, 1)
    cot_start = tied(cotangent, in_pieces[2], in_pieces[4])
    for k, step in steps.items():
        cot_pieces[k] = hop(tied(cot_start, in_pieces[6]) if k == 6 else cot_start, *step)
    in_pieces = [in_pieces[k] for k in range(8)]
    edges = (array(2, ncols, half),) * 2
    hidden, slope_one, *sent = expand((3, 5, 7), expand((2, 4, 6), first), edges=edges)
    hid_near, hid_far = meet(sent[0], 0), meet(sent[1], 1)

    mixed, slope_two = kernel(
        lambda *refs: middle_kernel(True, *refs), "inner", (full, array(nrows, ncols, half, dtype=F32)),
        (pos, taps, bd, hidden), [pad], **vpu,
    )
    mixed, slope_two = kernel(
        lambda *refs: middle_kernel(False, *refs), "outer", (full, array(nrows, ncols, half, dtype=F32)),
        (pos, taps, bd, hidden, hid_near, hid_far), [pad], into=(mixed, slope_two), **vpu,
    )
    for k in steps:
        cot_pieces[k + 1] = hop(tied(cot_pieces[k], mixed), 0, 1)

    def project(order, into=(), after=(), edges=()):
        return kernel(
            lambda *refs: project_kernel(order, *refs), "project%d" % order[0], (full,) + edges,
            (pos, w2, slope_two, *(cot_pieces[k] for k in order)), into=into, after=after, **mm,
        )

    def chunk_outs(rows, width):
        return (array(rows, width, dtype=F32),) + (array(rows, width),) * (groups - 1)

    half_done = project((0, 1, 2, 4, 6))
    w2_chunks = kernel(
        w2_kernel, "w2", chunk_outs(half // groups, cin), (pos, mixed, *(cot_pieces[k] for k in range(8))),
        [pltpu.VMEM((half, cin), F32)], after=half_done, **mm,
    )
    grad_pre, *sent = project((3, 5, 7), half_done, (w2_chunks[0],), edges)
    gp_near, gp_far = meet(sent[0], 0), meet(sent[1], 1)
    tail = 16 * groups
    small = kernel(
        taps_kernel, "taps", array(tail, half, dtype=F32), (pos, hidden, hid_near, hid_far, grad_pre),
        [pad, pltpu.VMEM((nrows, ncols, LANES), F32)], **vpu,
    )
    four = groups == 4
    w2_halves = halved(w2_chunks) if four else w2_chunks[:1]
    grad_act, grad_b1 = kernel(
        back_kernel, "back", (full, array(1, half, dtype=F32)),
        (pos, taps, grad_pre, gp_near, gp_far, slope_one), [pad, pltpu.VMEM((8, LANES), F32)],
        after=(small, *w2_halves), **vpu,
    )
    if four:
        w2_sent = hop(tied(w2_halves[1], small).astype(BF), 4, 0).astype(F32)
        w2_chunk = (tied(w2_halves[0], grad_act) + w2_sent).astype(BF)
    else:
        w2_chunk = summed(tied(w2_chunks[0], grad_act), w2_chunks[1:])
    w2_pair = jnp.stack([w2_chunk, hop(w2_chunk, 1, 0)])

    block = (own_rows, ncols, cin)
    two = (2, *block)
    to_core = kernel(core_kernel, "core", array(4, *block), (pos, grad_act, w1), after=(w2_chunk,), **mm)
    from_core = hop(to_core, 0, 1)
    w1_own, *w1_sends = kernel(
        w1_kernel, "w1", chunk_outs((cin + tail) // groups, half), (pos, grad_act, small, grad_b1, *in_pieces),
        [pltpu.VMEM((cin + tail, half), F32)], after=(w2_chunk, to_core), **mm,
    )
    going = kernel(
        chip_send_kernel, "chip_send", array(*two), (pos, grad_act, w1, from_core), after=(w1_own,), **mm
    )
    w2_pair = tied(w2_pair, going)
    if four:
        w2_quad = jnp.stack([w2_pair, hop(w2_pair, 4, 0)])
        w2_all = (w2_quad, hop(w2_quad, 2, 0))
    else:
        w2_all = [(hop(w2_pair, 2 * k, 0) if k else w2_pair)[None] for k in range(groups)]
    arrived = cross(going, 0)
    kept = kernel(
        chip_keep_kernel, "chip_keep", array(*two, dtype=F32), (pos, grad_act, w1, from_core), after=(going,), **mm
    )
    forward = kernel(forward_kernel, "forward", array(*block), (pos, kept, arrived), **mm)
    onward = cross(forward, 1)

    w1_chunk = summed(tied(w1_own, kept), w1_sends)
    w1_col = column(pos, w1_chunk, groups)
    line = array(1, hslice, dtype=F32)
    input_grad, out_w2, out_w1, out_k, out_bd, out_b1 = kernel(
        last_kernel, "last",
        (array(*block), array(hslice, cin, dtype=F32), array(cin, hslice, dtype=F32), array(25, hslice, dtype=F32), line, line),
        (pos, cot_own, kept, arrived, onward, w1_col, hop(w1_col, 1, 0), *w2_all),
        [pltpu.VMEM((tail, hslice), F32)],
    )
    return (input_grad, out_w1, out_b1.reshape(hslice), out_k, out_bd.reshape(hslice), out_w2)


def solution(mesh):
    in_specs = (
        P(("dp", "chan"), None, None),
        P(("dp", "chan"), None, None),
        P(None, "chan"),
        P("chan"),
        P(None, "chan"),
        P("chan"),
        P("chan", None),
    )
    out_specs = (
        P(("dp", "chan"), None, None),
        P(None, "chan"),
        P("chan"),
        P(None, "chan"),
        P("chan"),
        P("chan", None),
    )
    return jax.shard_map(shards, mesh=mesh, in_specs=in_specs, out_specs=out_specs, check_vma=False)
```

```python
import jax
import jax.numpy as jnp
from jax import lax
from jax.experimental import pallas as pl
from jax.experimental.pallas import tpu as pltpu
from jax.sharding import PartitionSpec as P

BF = jnp.bfloat16
F32 = jnp.float32
AXES = ("dp", "chan")
VMEM = pl.BlockSpec(memory_space=pltpu.VMEM)
SMEM = pl.BlockSpec(memory_space=pltpu.SMEM)
ANY = pl.BlockSpec(memory_space=pl.ANY)
EDGE = 8
LANES = 128
ROOM = 0


def array(*shape, dtype=BF):
    return jax.ShapeDtypeStruct(shape, dtype)


def kernel(body, name, out, args, scratch=(), flops=0, nbytes=0, after=(), into=()):
    first, last = len(args), len(args) + len(after) + len(into)

    def run(*refs):
        body(*refs[:first], *refs[last:])

    return pl.pallas_call(
        run,
        out_shape=out,
        in_specs=[SMEM] + [VMEM] * (len(args) - 1) + [ANY] * len(after) + [VMEM] * len(into),
        out_specs=jax.tree.map(lambda _: VMEM, out),
        scratch_shapes=list(scratch),
        compiler_params=pltpu.CompilerParams(vmem_limit_bytes=16 * 1024 * 1024),
        cost_estimate=pl.CostEstimate(flops=flops, bytes_accessed=nbytes, transcendentals=0),
        input_output_aliases={len(args) + len(after) + i: i for i in range(len(into))},
        name=name,
    )(*args, *after, *into)


def gelu_parts(pre):
    cdf = 0.5 * (1.0 + lax.erf(pre * 0.7071067811865476))
    dens = jnp.exp(-0.5 * pre * pre) * 0.3989422804014327
    return pre * cdf, cdf + pre * dens


def hop(value, dp_xor, chan_xor):
    ndp, nchan = lax.axis_size("dp"), lax.axis_size("chan")
    pairs = [
        (d * nchan + c, (d ^ dp_xor) * nchan + (c ^ chan_xor))
        for d in range(ndp)
        for c in range(nchan)
    ]
    return lax.ppermute(value, AXES, pairs)


def cross(value, turn):
    ndp, nchan = lax.axis_size("dp"), lax.axis_size("chan")
    pairs = []
    for d in range(ndp):
        for c in range(nchan):
            to = (d ^ 1, c) if (c & 1) == turn else (d, c ^ 2)
            pairs.append((d * nchan + c, to[0] * nchan + to[1]))
    return lax.ppermute(value, AXES, pairs)


def meet(value, odd):
    ndp, nchan = lax.axis_size("dp"), lax.axis_size("chan")
    pairs = []
    for d in range(ndp):
        to = d + 2 if (d // 2) % 2 == odd else d - 2
        if 0 <= to < ndp:
            pairs += [(d * nchan + c, to * nchan + c) for c in range(nchan)]
    return lax.ppermute(value, AXES, pairs)


def tied(value, *others):
    return lax.optimization_barrier((value, *others))[0]


def prepare_kernel(pos, w1, b1, taps, b2, w2, rows, cot, w1_own, b1_own, taps_own, b2_own, w2_own, rows_own, cot_own, *pads):
    half = b1_own.shape[1]
    cut = pl.ds(pl.multiple_of(pos[1] * half, half), half)
    w1_own[...] = w1[:, cut]
    b1_own[...] = b1[:, cut]
    taps_own[...] = taps[:, cut]
    b2_own[...] = b2[:, cut]
    w2_own[...] = w2[cut, :]
    rows_own[...] = rows[...]
    cot_own[...] = cot[...]
    for pad in pads:
        zeros = jnp.zeros((pad.shape[0], pad.shape[1], EDGE, LANES), F32)
        pad[:, :, 0:EDGE, :] = zeros
        pad[:, :, pad.shape[2] - EDGE :, :] = zeros


def cuts(half):
    return [(c, slice(c * LANES, (c + 1) * LANES)) for c in range(half // LANES)]


def put_rows(pad, at, value):
    rows, ncols, half = value.shape
    value = value.astype(BF).astype(F32)
    for c, cut in cuts(half):
        pad[c, pl.ds(at + 2, rows), EDGE : EDGE + ncols, :] = value[:, :, cut]


def put_edges(pos, pad, edges):
    _, ncols, half = edges[0].shape
    last = pad.shape[1] - 6
    odd = pos[2] & 1
    for edge, at in zip(edges, (last * (1 - odd), last * odd)):
        for c, cut in cuts(half):
            edge[:, :, cut] = pad[c, pl.ds(at + 2, 2), EDGE : EDGE + ncols, :].astype(BF)


def put_halo(pos, pad, near, far):
    _, ncols, half = near.shape
    last = pad.shape[1] - 2
    odd = pos[2] & 1
    for edge, at in zip((near, far), (last * (1 - odd), last * odd)):
        for c, cut in cuts(half):
            pad[c, pl.ds(at, 2), EDGE : EDGE + ncols, :] = edge[:, :, cut].astype(F32)


def expand_kernel(order, pos, w, b, *refs):
    pieces, (hid, slope, *edges, pre) = refs[: len(order)], refs[len(order) :]
    n, ncols, cin = pieces[0].shape
    half = slope.shape[2]
    for k, piece in zip(order, pieces):
        at = (pos[0] ^ k) * n
        pre[...] = (
            jnp.dot(piece[...].reshape(n * ncols, cin), w[...], preferred_element_type=F32) + b[...]
        ).reshape(n, ncols, half)

        def body(r, carry, at=at):
            h, s = gelu_parts(pre[pl.ds(r, 1)])
            put_rows(hid, at + r, h)
            slope[pl.ds(at + r, 1)] = s.astype(BF)
            return carry

        lax.fori_loop(0, n, body, 0)
    if edges:
        put_edges(pos, hid, edges)


def conv_tiles(pad, taps, cut, ncols, starts, nr, cols, flip, emit):
    def body(i, carry):
        w0 = i * cols
        for r0 in starts:
            acc = [None] * nr
            for j in range(5):
                xs = [pad[r0 + q, pl.ds(w0 + (EDGE - 2) + j, cols), :] for q in range(nr + 4)]
                for q in range(5):
                    t = 5 * q + j
                    t = 24 - t if flip else t
                    for r in range(nr):
                        term = taps[t : t + 1, cut] * xs[r + q]
                        acc[r] = term if acc[r] is None else acc[r] + term
            emit(r0, pl.ds(pl.multiple_of(w0, cols), cols), acc)
        return carry

    lax.fori_loop(0, ncols // cols, body, 0)


def middle_kernel(inner, pos, taps, bias, *refs):
    if inner:
        pad, mixed, slope = refs
    else:
        near, far, mixed, slope, pad = refs
        put_halo(pos, pad, near, far)
    nrows, ncols, half = mixed.shape
    for c, cut in cuts(half):
        add = bias[:, cut]

        def emit(r0, w, acc, cut=cut, add=add):
            for r in range(len(acc)):
                m, s = gelu_parts(acc[r] + add)
                mixed[r0 + r, w, cut] = m.astype(BF)
                slope[r0 + r, w, cut] = s

        if inner:
            conv_tiles(pad.at[c], taps, cut, ncols, range(2, nrows - 2, 4), 4, 16, False, emit)
        else:
            conv_tiles(pad.at[c], taps, cut, ncols, (0, nrows - 2), 2, 32, False, emit)


def project_kernel(order, pos, weights, slope, *refs):
    pieces, (gp, *edges) = refs[: len(order)], refs[len(order) :]
    n, ncols, cin = pieces[0].shape
    half = slope.shape[2]
    for k, piece in zip(order, pieces):
        at = (pos[0] ^ k) * n
        res = lax.dot_general(
            piece[...].reshape(n * ncols, cin), weights[...], (((1,), (1,)), ((), ())), preferred_element_type=F32
        )
        put_rows(gp, at, res.reshape(n, ncols, half) * slope[pl.ds(at, n)])
    if edges:
        put_edges(pos, gp, edges)


def outer_sum(pos, total, pieces, values, swap):
    n, ncols, _ = pieces[0].shape
    for k, piece in enumerate(pieces):
        a = piece[...].reshape(n * ncols, -1)
        b = values[pl.ds((pos[0] ^ k) * n, n)].reshape(n * ncols, -1)
        if swap:
            a, b = b, a
        part = lax.dot_general(a, b, (((0,), (0,)), ((), ())), preferred_element_type=F32)
        if k == 0:
            total[0 : part.shape[0], :] = part
        else:
            total[0 : part.shape[0], :] += part


def w2_kernel(pos, mixed, *refs):
    pieces, outs, total = refs[:8], refs[8:-1], refs[-1]
    outer_sum(pos, total, pieces, mixed, True)
    n = outs[0].shape[0]
    for k, ref in enumerate(outs):
        ref[...] = total[pl.ds(pl.multiple_of((pos[2] ^ k) * n, n), n), :].astype(ref.dtype)


def taps_kernel(pos, hid, gp, small):
    _, nrows, ncols, _ = hid.shape
    nrows, ncols = nrows - 4, ncols - 2 * EDGE
    small[...] = jnp.zeros_like(small)
    for c, cut in cuts(small.shape[1]):

        def body(i, accs, c=c):
            accs = list(accs)
            w0 = i * 8
            for j in range(5):
                xs = [hid[c, q, pl.ds(w0 + (EDGE - 2) + j, 8), :] for q in range(4)]
                for r in range(nrows):
                    xs.append(hid[c, r + 4, pl.ds(w0 + (EDGE - 2) + j, 8), :])
                    g = gp[c, r + 2, pl.ds(pl.multiple_of(w0 + EDGE, 8), 8), :]
                    for q in range(5):
                        accs[5 * q + j] = accs[5 * q + j] + xs[r + q] * g
                    if j == 0:
                        accs[25] = accs[25] + g
            return tuple(accs)

        zero = jnp.zeros((8, LANES), F32)
        accs = lax.fori_loop(0, ncols // 8, body, (zero,) * 26)
        for t in range(26):
            small[t : t + 1, cut] = jnp.sum(accs[t], axis=0, keepdims=True)


def back_kernel(pos, taps, near, far, slope, pad, act, grad_b, total):
    nrows, ncols, half = act.shape
    put_halo(pos, pad, near, far)
    for c, cut in cuts(half):
        total[...] = jnp.zeros_like(total)

        def emit(r0, w, acc, cut=cut):
            part = jnp.zeros((8, LANES), F32)
            for r in range(4):
                a = (acc[r] * slope[r0 + r, w, cut].astype(F32)).astype(BF)
                act[r0 + r, w, cut] = a
                part = part + jnp.sum(a.astype(F32).reshape(-1, 8, LANES), axis=0)
            total[...] += part

        conv_tiles(pad.at[c], taps, cut, ncols, range(0, nrows, 4), 4, 16, True, emit)
        grad_b[:, cut] = jnp.sum(total[...], axis=0, keepdims=True)


def w1_kernel(pos, act, small, grad_b, *refs):
    pieces, outs, total = refs[:8], refs[8:-1], refs[-1]
    outer_sum(pos, total, pieces, act, False)
    cin = pieces[0].shape[2]
    total[cin:, :] = small[...]
    total[cin + 26 : cin + 27, :] = grad_b[...]
    chunks = len(outs)
    n, m = cin // chunks, small.shape[0] // chunks
    for k, ref in enumerate(outs):
        at = pos[2] ^ k
        ref[0:n, :] = total[pl.ds(pl.multiple_of(at * n, n), n), :].astype(ref.dtype)
        ref[n:, :] = total[pl.ds(pl.multiple_of(cin + at * m, m), m), :].astype(ref.dtype)


def share(pos, act, w, chip_xor, core):
    ncols, half = act.shape[1:]
    n = act.shape[0] // 8
    at = (((pos[0] // 2) ^ chip_xor) * 2 + core) * n
    return lax.dot_general(
        act[pl.ds(at, n)].reshape(n * ncols, half), w[...], (((1,), (1,)), ((), ())), preferred_element_type=F32
    ).reshape(n, ncols, -1)


def core_kernel(pos, act, w, out):
    for k in range(4):
        out[k] = share(pos, act, w, k, 1 - pos[3]).astype(BF)


def chip_send_kernel(pos, act, w, other, out):
    for i, k in enumerate((2 - pos[3], 3)):
        out[i] = (share(pos, act, w, k, pos[3]) + other[k].astype(F32)).astype(BF)


def chip_keep_kernel(pos, act, w, other, out):
    for i, k in enumerate((0, 1 + pos[3])):
        out[i] = share(pos, act, w, k, pos[3]) + other[k].astype(F32)


def forward_kernel(pos, kept, arrived, out):
    out[...] = (kept[1] + arrived[1].astype(F32)).astype(BF)


def finish_kernel(pos, cot, kept, arrived, last, out):
    out[...] = (cot[...].astype(F32) + (kept[0] + arrived[0].astype(F32) + last[...].astype(F32))).astype(BF)


def sum_kernel(pos, own, *refs):
    total = own[...]
    for part in refs[:-1]:
        total = total + part[...].astype(F32)
    refs[-1][...] = total.astype(BF)


def copy_kernel(pos, value, out):
    out[...] = value[...]


def column_kernel(pos, *refs):
    blocks, out = refs[:-1], refs[-1]
    n = blocks[0].shape[0]
    for k, block in enumerate(blocks):
        out[pos[2] ^ k, 0:n] = block[...]
        if n < out.shape[1]:
            out[pos[2] ^ k, n:] = jnp.zeros((out.shape[1] - n, out.shape[2]), out.dtype)


def w2_place_kernel(pos, mine, other, out):
    g, _, cin = mine.shape
    n = out.shape[0] // (2 * g)
    for k, col in enumerate((mine, other)):
        for i in range(g):
            out[pl.ds(pl.multiple_of(((pos[1] ^ k) * g + i) * n, n), n), :] = col[i, 0:n].astype(F32)


def w1_place_kernel(pos, blocks, out, grad_k, grad_bd, grad_b1, small):
    g = len(blocks) // 2
    half = blocks[0].shape[1]
    n = out.shape[0] // g
    m = small.shape[0] // g
    for i, block in enumerate(blocks):
        cut = pl.ds(pl.multiple_of((pos[1] ^ (i // g)) * half, half), half)
        at = pos[2] ^ (i % g)
        out[pl.ds(pl.multiple_of(at * n, n), n), cut] = block[0:n, :].astype(F32)
        small[pl.ds(pl.multiple_of(at * m, m), m), cut] = block[n:, :].astype(F32)
    grad_k[...] = small[0:25, :]
    grad_bd[...] = small[25:26, :]
    grad_b1[...] = small[26:27, :]


def last_kernel(pos, cot, kept, arrived, last, mine, other, *refs):
    blocks, (out, out_w2, out_w1, grad_k, grad_bd, grad_b1, small) = refs[:-7], refs[-7:]
    finish_kernel(pos, cot, kept, arrived, last, out)
    w2_place_kernel(pos, mine, other, out_w2)
    w1_place_kernel(pos, blocks, out_w1, grad_k, grad_bd, grad_b1, small)


def summed(own, sends):
    for k, send in enumerate(sends):
        own = own + hop(send, 2 * (k + 1), 0).astype(F32)
    return own.astype(BF)


def halved(chunks):
    arrived = hop(jnp.stack([chunks[1], chunks[3]]), 2, 0).astype(F32)
    return chunks[0] + arrived[0], chunks[2] + arrived[1]


def shards(inputs, cotangent, expand_w, expand_b, depth_k, depth_b, project_w):
    chan, dp = lax.axis_index("chan"), lax.axis_index("dp")
    pair, zpos = dp & 1, dp >> 1
    groups = lax.axis_size("dp") // 2
    own_rows, ncols, cin = inputs.shape
    nrows = 8 * own_rows
    hslice = expand_w.shape[1]
    half = hslice // 2
    npix = nrows * ncols
    pos = jnp.stack([pair * 4 + chan, pair, zpos, chan & 1]).astype(jnp.int32)

    full = array(nrows, ncols, half)
    mm = vpu = dict(flops=1024, nbytes=1024)
    long = dict(flops=2 * 10**10, nbytes=10**8)
    padded = array(half // LANES, nrows + 4, ncols + 2 * EDGE, LANES, dtype=F32)

    mine = array(*inputs.shape)
    w1, b1, taps, bd, w2, rows_own, cot_own, hidden, grad_pre = kernel(
        prepare_kernel, "prepare",
        (array(cin, half), array(1, half, dtype=F32), array(25, half, dtype=F32), array(1, half, dtype=F32),
         array(half, cin), mine, mine, padded, padded),
        (pos, expand_w, expand_b.reshape(1, hslice), depth_k, depth_b.reshape(1, hslice), project_w, inputs, cotangent),
    )

    def expand(order, into=(), after=(), edges=()):
        return kernel(
            lambda *refs: expand_kernel(order, *refs), "expand%d" % order[0], (padded, full) + edges,
            (pos, w1, b1, *(in_pieces[k] for k in order)), [pltpu.VMEM((own_rows, ncols, half), F32)],
            into=into, after=after, **mm,
        )

    in_pieces = {0: rows_own, 1: hop(inputs, 0, 1)}
    cot_pieces = {0: cot_own, 1: hop(cotangent, 0, 1)}
    steps = {4: (1, 0), 2: (0, 2), 6: (1, 2)}
    for k, step in steps.items():
        in_pieces[k] = hop(inputs, *step)
    first = expand((0, 1), (hidden,), after=(cot_pieces[1],))
    for k in steps:
        in_pieces[k + 1] = hop(tied(in_pieces[k], first[0]), 0, 1)
    second = expand((2, 4), first)
    cot_start = tied(cotangent, in_pieces[2], in_pieces[4], second[1])
    for k, step in steps.items():
        cot_pieces[k] = hop(tied(cot_start, in_pieces[6]) if k == 6 else cot_start, *step)
    in_pieces = [in_pieces[k] for k in range(8)]
    edges = (array(2, ncols, half),) * 2
    hidden, slope_one, *sent = expand((7,), expand((6, 3, 5), second), edges=edges)
    hid_near, hid_far = meet(sent[0], 0), meet(sent[1], 1)

    f32_full = array(nrows, ncols, half, dtype=F32)
    inner = kernel(
        lambda *refs: middle_kernel(True, *refs), "inner", (full, f32_full), (pos, taps, bd, hidden), **vpu
    )
    mixed, slope_two, hidden = kernel(
        lambda *refs: middle_kernel(False, *refs), "outer", (full, f32_full, padded),
        (pos, taps, bd, hid_near, hid_far), into=(*inner, hidden), **vpu,
    )
    for k in steps:
        cot_pieces[k + 1] = hop(tied(cot_pieces[k], mixed), 0, 1)

    def project(order, into=(), after=(), edges=()):
        return kernel(
            lambda *refs: project_kernel(order, *refs), "project%d" % order[0], (padded,) + edges,
            (pos, w2, slope_two, *(cot_pieces[k] for k in order)), into=into, after=after, **mm,
        )

    def chunk_outs(rows, width):
        return (array(rows, width, dtype=F32),) + (array(rows, width),) * (groups - 1)

    half_done = project((0, 1, 2, 4, 6), (grad_pre,))
    w2_chunks = kernel(
        w2_kernel, "w2", chunk_outs(half // groups, cin), (pos, mixed, *(cot_pieces[k] for k in range(8))),
        [pltpu.VMEM((half, cin), F32)], after=half_done, **mm,
    )
    grad_pre, *sent = project((3, 5, 7), half_done, (w2_chunks[0],), edges)
    gp_near, gp_far = meet(sent[0], 0), meet(sent[1], 1)
    tail = 16 * groups
    small = kernel(taps_kernel, "taps", array(tail, half, dtype=F32), (pos, hidden, grad_pre), **vpu)
    four = groups == 4
    w2_halves = halved(w2_chunks) if four else w2_chunks[:1]
    _, grad_act, grad_b1 = kernel(
        back_kernel, "back", (padded, full, array(1, half, dtype=F32)), (pos, taps, gp_near, gp_far, slope_one),
        [pltpu.VMEM((8, LANES), F32)], after=(small, *w2_halves), into=(grad_pre,), **vpu,
    )
    if four:
        w2_sent = hop(tied(w2_halves[1], small).astype(BF), 4, 0).astype(F32)
        w2_chunk = (tied(w2_halves[0], grad_act) + w2_sent).astype(BF)
    else:
        w2_chunk = summed(tied(w2_chunks[0], grad_act), w2_chunks[1:])
    w2_two = jnp.stack([w2_chunk, hop(w2_chunk, 4, 0)]) if four else None

    block = (own_rows, ncols, cin)
    two = (2, *block)
    to_core = kernel(core_kernel, "core", array(4, *block), (pos, grad_act, w1), after=(w2_chunk,), **mm)
    from_core = hop(to_core, 0, 1)
    w1_own, *w1_sends = kernel(
        w1_kernel, "w1", chunk_outs((cin + tail) // groups, half), (pos, grad_act, small, grad_b1, *in_pieces),
        [pltpu.VMEM((cin + tail, half), F32)], after=(w2_chunk, to_core), **mm,
    )
    going = kernel(
        chip_send_kernel, "chip_send", array(*two), (pos, grad_act, w1, from_core), after=(w1_own,), **mm
    )
    if four:
        w2_far = hop(tied(w2_two, going), 2, 0)
        w2_blocks = [w2_two[0], w2_far[0], w2_two[1], w2_far[1]]
    else:
        w2_blocks = [hop(w2_chunk, 2 * k, 0) if k else w2_chunk for k in range(groups)]
    arrived = cross(going, 0)
    w1_parts = [hop(send, 2 * (k + 1), 0) for k, send in enumerate(w1_sends)]
    w1_chunk = kernel(sum_kernel, "sum", array(*w1_own.shape), (pos, w1_own, *w1_parts), after=(going,), **long)
    w1_side = hop(w1_chunk, 1, 0)
    w1_near = [hop(w1_chunk, 2 * k, 0) if k else w1_chunk for k in range(groups)]
    kept = kernel(
        chip_keep_kernel, "chip_keep", array(*two, dtype=F32), (pos, grad_act, w1, from_core), after=(w1_chunk,), **mm
    )
    w2_col = kernel(
        column_kernel, "column", array(groups, half // groups + ROOM, cin), (pos, *w2_blocks), after=(kept,), **mm
    )
    w2_other = hop(w2_col, 1, 0)
    forward = kernel(forward_kernel, "forward", array(*block), (pos, kept, arrived), **mm)
    onward = cross(forward, 1)
    w1_side = kernel(copy_kernel, "side", array(*w1_side.shape), (pos, w1_side), after=(w1_near[-1],), **long)
    w1_blocks = w1_near + [hop(w1_side, 2 * k, 0) if k else w1_side for k in range(groups)]
    line = array(1, hslice, dtype=F32)
    input_grad, out_w2, out_w1, out_k, out_bd, out_b1 = kernel(
        last_kernel, "last",
        (array(*block), array(hslice, cin, dtype=F32), array(cin, hslice, dtype=F32), array(25, hslice, dtype=F32), line, line),
        (pos, cot_own, kept, arrived, onward, w2_col, w2_other, *w1_blocks),
        [pltpu.VMEM((tail, hslice), F32)],
    )
    return (input_grad, out_w1, out_b1.reshape(hslice), out_k, out_bd.reshape(hslice), out_w2)


def solution(mesh):
    in_specs = (
        P(("dp", "chan"), None, None),
        P(("dp", "chan"), None, None),
        P(None, "chan"),
        P("chan"),
        P(None, "chan"),
        P("chan"),
        P("chan", None),
    )
    out_specs = (
        P(("dp", "chan"), None, None),
        P(None, "chan"),
        P("chan"),
        P(None, "chan"),
        P("chan"),
        P("chan", None),
    )
    return jax.shard_map(shards, mesh=mesh, in_specs=in_specs, out_specs=out_specs, check_vma=False)
```

```python
import jax
import jax.numpy as jnp
from jax import lax
from jax.experimental import pallas as pl
from jax.experimental.pallas import tpu as pltpu
from jax.sharding import PartitionSpec as P

BF = jnp.bfloat16
F32 = jnp.float32
AXES = ("dp", "chan")
VMEM = pl.BlockSpec(memory_space=pltpu.VMEM)
SMEM = pl.BlockSpec(memory_space=pltpu.SMEM)
ANY = pl.BlockSpec(memory_space=pl.ANY)
EDGE = 8
LANES = 128
FLIP_HID, FLIP_GP = 0, 1
FIRST = 2
ROOM = 0


def array(*shape, dtype=BF):
    return jax.ShapeDtypeStruct(shape, dtype)


def kernel(body, name, out, args, scratch=(), flops=0, nbytes=0, after=(), into=()):
    first, last = len(args), len(args) + len(after) + len(into)

    def run(*refs):
        body(*refs[:first], *refs[last:])

    return pl.pallas_call(
        run,
        out_shape=out,
        in_specs=[SMEM] + [VMEM] * (len(args) - 1) + [ANY] * len(after) + [VMEM] * len(into),
        out_specs=jax.tree.map(lambda _: VMEM, out),
        scratch_shapes=list(scratch),
        compiler_params=pltpu.CompilerParams(vmem_limit_bytes=16 * 1024 * 1024),
        cost_estimate=pl.CostEstimate(flops=flops, bytes_accessed=nbytes, transcendentals=0),
        input_output_aliases={len(args) + len(after) + i: i for i in range(len(into))},
        name=name,
    )(*args, *after, *into)


def gelu_parts(pre):
    cdf = 0.5 * (1.0 + lax.erf(pre * 0.7071067811865476))
    dens = jnp.exp(-0.5 * pre * pre) * 0.3989422804014327
    return pre * cdf, cdf + pre * dens


def hop(value, dp_xor, chan_xor):
    ndp, nchan = lax.axis_size("dp"), lax.axis_size("chan")
    pairs = [
        (d * nchan + c, (d ^ dp_xor) * nchan + (c ^ chan_xor))
        for d in range(ndp)
        for c in range(nchan)
    ]
    return lax.ppermute(value, AXES, pairs)


def cross(value, turn):
    ndp, nchan = lax.axis_size("dp"), lax.axis_size("chan")
    pairs = []
    for d in range(ndp):
        for c in range(nchan):
            to = (d ^ 1, c) if (c & 1) == turn else (d, c ^ 2)
            pairs.append((d * nchan + c, to[0] * nchan + to[1]))
    return lax.ppermute(value, AXES, pairs)


def meet(value, odd):
    ndp, nchan = lax.axis_size("dp"), lax.axis_size("chan")
    pairs = []
    for d in range(ndp):
        to = d + 2 if (d // 2) % 2 == odd else d - 2
        if 0 <= to < ndp:
            pairs += [(d * nchan + c, to * nchan + c) for c in range(nchan)]
    return lax.ppermute(value, AXES, pairs)


def tied(value, *others):
    return lax.optimization_barrier((value, *others))[0]


def prepare_kernel(pos, w1, b1, taps, b2, w2, rows, cot, w1_own, b1_own, taps_own, b2_own, w2_own, rows_own, cot_own, *pads):
    half = b1_own.shape[1]
    cut = pl.ds(pl.multiple_of(pos[1] * half, half), half)
    w1_own[...] = w1[:, cut]
    b1_own[...] = b1[:, cut]
    taps_own[...] = taps[:, cut]
    b2_own[...] = b2[:, cut]
    w2_own[...] = w2[cut, :]
    rows_own[...] = rows[...]
    cot_own[...] = cot[...]
    for pad in pads:
        zeros = jnp.zeros((pad.shape[0], pad.shape[1], EDGE, LANES), F32)
        pad[:, :, 0:EDGE, :] = zeros
        pad[:, :, pad.shape[2] - EDGE :, :] = zeros


def cuts(half):
    return [(c, slice(c * LANES, (c + 1) * LANES)) for c in range(half // LANES)]


def put_rows(pad, at, value):
    rows, ncols, half = value.shape
    value = value.astype(BF).astype(F32)
    for c, cut in cuts(half):
        pad[c, pl.ds(at + 2, rows), EDGE : EDGE + ncols, :] = value[:, :, cut]


def put_edges(pos, pad, edges, flip):
    _, ncols, half = edges[0].shape
    last = pad.shape[1] - 6
    odd = (pos[2] & 1) ^ flip
    for edge, at in zip(edges, (last * (1 - odd), last * odd)):
        for c, cut in cuts(half):
            edge[:, :, cut] = pad[c, pl.ds(at + 2, 2), EDGE : EDGE + ncols, :].astype(BF)


def put_halo(pos, pad, near, far, flip):
    _, ncols, half = near.shape
    last = pad.shape[1] - 2
    odd = (pos[2] & 1) ^ flip
    for edge, at in zip((near, far), (last * (1 - odd), last * odd)):
        for c, cut in cuts(half):
            pad[c, pl.ds(at, 2), EDGE : EDGE + ncols, :] = edge[:, :, cut].astype(F32)


def expand_kernel(order, pos, w, b, *refs):
    pieces, (hid, slope, *edges, pre) = refs[: len(order)], refs[len(order) :]
    n, ncols, cin = pieces[0].shape
    half = slope.shape[2]
    for k, piece in zip(order, pieces):
        at = (pos[0] ^ k) * n
        pre[...] = (
            jnp.dot(piece[...].reshape(n * ncols, cin), w[...], preferred_element_type=F32) + b[...]
        ).reshape(n, ncols, half)

        def body(r, carry, at=at):
            h, s = gelu_parts(pre[pl.ds(r, 1)])
            put_rows(hid, at + r, h)
            slope[pl.ds(at + r, 1)] = s.astype(BF)
            return carry

        lax.fori_loop(0, n, body, 0)
    if edges:
        put_edges(pos, hid, edges, FLIP_HID)


def conv_tiles(pad, taps, cut, ncols, starts, nr, cols, flip, emit):
    def body(i, carry):
        w0 = i * cols
        for r0 in starts:
            acc = [None] * nr
            for j in range(5):
                xs = [pad[r0 + q, pl.ds(w0 + (EDGE - 2) + j, cols), :] for q in range(nr + 4)]
                for q in range(5):
                    t = 5 * q + j
                    t = 24 - t if flip else t
                    for r in range(nr):
                        term = taps[t : t + 1, cut] * xs[r + q]
                        acc[r] = term if acc[r] is None else acc[r] + term
            emit(r0, pl.ds(pl.multiple_of(w0, cols), cols), acc)
        return carry

    lax.fori_loop(0, ncols // cols, body, 0)


def middle_kernel(inner, pos, taps, bias, *refs):
    if inner:
        pad, mixed, slope = refs
    else:
        near, far, mixed, slope, pad = refs
        put_halo(pos, pad, near, far, FLIP_HID)
    nrows, ncols, half = mixed.shape
    for c, cut in cuts(half):
        add = bias[:, cut]

        def emit(r0, w, acc, cut=cut, add=add):
            for r in range(len(acc)):
                m, s = gelu_parts(acc[r] + add)
                mixed[r0 + r, w, cut] = m.astype(BF)
                slope[r0 + r, w, cut] = s

        if inner:
            conv_tiles(pad.at[c], taps, cut, ncols, range(2, nrows - 2, 4), 4, 16, False, emit)
        else:
            conv_tiles(pad.at[c], taps, cut, ncols, (0, nrows - 2), 2, 32, False, emit)


def cot_blocks(pos, which, refs):
    core = pos[3]
    found = []
    for i, ref in zip(which, refs):
        if i in (2, 4):
            found += [((4 - 2 * core if i == 2 else 3 + 2 * core) + (j if i == 2 else -j), ref.at[j]) for j in range(2)]
        else:
            found.append(({0: 0, 1: 1, 3: 6, 5: 7}[i], ref))
    return found


def project_kernel(which, pos, weights, slope, *refs):
    pieces, (gp, *edges) = cot_blocks(pos, which, refs[: len(which)]), refs[len(which) :]
    n, ncols, cin = pieces[0][1].shape
    half = slope.shape[2]
    for k, piece in pieces:
        at = (pos[0] ^ k) * n
        res = lax.dot_general(
            piece[...].reshape(n * ncols, cin), weights[...], (((1,), (1,)), ((), ())), preferred_element_type=F32
        )
        put_rows(gp, at, res.reshape(n, ncols, half) * slope[pl.ds(at, n)])
    if edges:
        put_edges(pos, gp, edges, FLIP_GP)


def outer_sum(pos, total, pieces, values, swap):
    n, ncols, _ = pieces[0][1].shape
    for i, (k, piece) in enumerate(pieces):
        a = piece[...].reshape(n * ncols, -1)
        b = values[pl.ds((pos[0] ^ k) * n, n)].reshape(n * ncols, -1)
        if swap:
            a, b = b, a
        part = lax.dot_general(a, b, (((0,), (0,)), ((), ())), preferred_element_type=F32)
        if i == 0:
            total[0 : part.shape[0], :] = part
        else:
            total[0 : part.shape[0], :] += part


def w2_kernel(pos, mixed, *refs):
    pieces, outs, total = cot_blocks(pos, range(6), refs[:6]), refs[6:-1], refs[-1]
    outer_sum(pos, total, pieces, mixed, True)
    n = outs[0].shape[0]
    for k, ref in enumerate(outs):
        ref[...] = total[pl.ds(pl.multiple_of((pos[2] ^ k) * n, n), n), :].astype(ref.dtype)


def taps_kernel(pos, hid, gp, small):
    _, nrows, ncols, _ = hid.shape
    nrows, ncols = nrows - 4, ncols - 2 * EDGE
    small[...] = jnp.zeros_like(small)
    for c, cut in cuts(small.shape[1]):

        def body(i, accs, c=c):
            accs = list(accs)
            w0 = i * 8
            for j in range(5):
                xs = [hid[c, q, pl.ds(w0 + (EDGE - 2) + j, 8), :] for q in range(4)]
                for r in range(nrows):
                    xs.append(hid[c, r + 4, pl.ds(w0 + (EDGE - 2) + j, 8), :])
                    g = gp[c, r + 2, pl.ds(pl.multiple_of(w0 + EDGE, 8), 8), :]
                    for q in range(5):
                        accs[5 * q + j] = accs[5 * q + j] + xs[r + q] * g
                    if j == 0:
                        accs[25] = accs[25] + g
            return tuple(accs)

        zero = jnp.zeros((8, LANES), F32)
        accs = lax.fori_loop(0, ncols // 8, body, (zero,) * 26)
        for t in range(26):
            small[t : t + 1, cut] = jnp.sum(accs[t], axis=0, keepdims=True)


def back_kernel(pos, taps, near, far, slope, pad, act, grad_b, total):
    nrows, ncols, half = act.shape
    put_halo(pos, pad, near, far, FLIP_GP)
    for c, cut in cuts(half):
        total[...] = jnp.zeros_like(total)

        def emit(r0, w, acc, cut=cut):
            part = jnp.zeros((8, LANES), F32)
            for r in range(4):
                a = (acc[r] * slope[r0 + r, w, cut].astype(F32)).astype(BF)
                act[r0 + r, w, cut] = a
                part = part + jnp.sum(a.astype(F32).reshape(-1, 8, LANES), axis=0)
            total[...] += part

        conv_tiles(pad.at[c], taps, cut, ncols, range(0, nrows, 4), 4, 16, True, emit)
        grad_b[:, cut] = jnp.sum(total[...], axis=0, keepdims=True)


def w1_kernel(pos, act, small, grad_b, *refs):
    pieces, outs, total = refs[:8], refs[8:-1], refs[-1]
    outer_sum(pos, total, list(enumerate(pieces)), act, False)
    cin = pieces[0].shape[2]
    total[cin:, :] = small[...]
    total[cin + 26 : cin + 27, :] = grad_b[...]
    chunks = len(outs)
    n, m = cin // chunks, small.shape[0] // chunks
    for k, ref in enumerate(outs):
        at = pos[2] ^ k
        ref[0:n, :] = total[pl.ds(pl.multiple_of(at * n, n), n), :].astype(ref.dtype)
        ref[n:, :] = total[pl.ds(pl.multiple_of(cin + at * m, m), m), :].astype(ref.dtype)


def share(pos, act, w, chip_xor, core):
    ncols, half = act.shape[1:]
    n = act.shape[0] // 8
    at = (((pos[0] // 2) ^ chip_xor) * 2 + core) * n
    return lax.dot_general(
        act[pl.ds(at, n)].reshape(n * ncols, half), w[...], (((1,), (1,)), ((), ())), preferred_element_type=F32
    ).reshape(n, ncols, -1)


def core_kernel(pos, act, w, out):
    for k in range(4):
        out[k] = share(pos, act, w, k, 1 - pos[3]).astype(BF)


def chip_send_kernel(pos, act, w, other, out):
    for i, k in enumerate((2 - pos[3], 3)):
        out[i] = (share(pos, act, w, k, pos[3]) + other[k].astype(F32)).astype(BF)


def chip_keep_kernel(pos, act, w, other, out):
    for i, k in enumerate((0, 1 + pos[3])):
        out[i] = share(pos, act, w, k, pos[3]) + other[k].astype(F32)


def forward_kernel(pos, kept, arrived, out):
    out[...] = (kept[1] + arrived[1].astype(F32)).astype(BF)


def finish_kernel(pos, cot, kept, arrived, last, out):
    out[...] = (cot[...].astype(F32) + (kept[0] + arrived[0].astype(F32) + last[...].astype(F32))).astype(BF)


def sum_kernel(pos, own, *refs):
    total = own[...]
    for part in refs[:-1]:
        total = total + part[...].astype(F32)
    refs[-1][...] = total.astype(BF)


def copy_kernel(pos, value, out):
    out[...] = value[...]


def column_kernel(pos, *refs):
    blocks, out = refs[:-1], refs[-1]
    n = blocks[0].shape[0]
    for k, block in enumerate(blocks):
        out[pos[2] ^ k, 0:n] = block[...]
        if n < out.shape[1]:
            out[pos[2] ^ k, n:] = jnp.zeros((out.shape[1] - n, out.shape[2]), out.dtype)


def w2_place_kernel(pos, mine, other, out):
    g, _, cin = mine.shape
    n = out.shape[0] // (2 * g)
    for k, col in enumerate((mine, other)):
        for i in range(g):
            out[pl.ds(pl.multiple_of(((pos[1] ^ k) * g + i) * n, n), n), :] = col[i, 0:n].astype(F32)


def w1_place_kernel(pos, blocks, out, grad_k, grad_bd, grad_b1, small):
    g = len(blocks) // 2
    half = blocks[0].shape[1]
    n = out.shape[0] // g
    m = small.shape[0] // g
    for i, block in enumerate(blocks):
        cut = pl.ds(pl.multiple_of((pos[1] ^ (i // g)) * half, half), half)
        at = pos[2] ^ (i % g)
        out[pl.ds(pl.multiple_of(at * n, n), n), cut] = block[0:n, :].astype(F32)
        small[pl.ds(pl.multiple_of(at * m, m), m), cut] = block[n:, :].astype(F32)
    grad_k[...] = small[0:25, :]
    grad_bd[...] = small[25:26, :]
    grad_b1[...] = small[26:27, :]


def last_kernel(pos, cot, kept, arrived, last, mine, other, *refs):
    blocks, (out, out_w2, out_w1, grad_k, grad_bd, grad_b1, small) = refs[:-7], refs[-7:]
    finish_kernel(pos, cot, kept, arrived, last, out)
    w2_place_kernel(pos, mine, other, out_w2)
    w1_place_kernel(pos, blocks, out_w1, grad_k, grad_bd, grad_b1, small)


def summed(own, sends):
    for k, send in enumerate(sends):
        own = own + hop(send, 2 * (k + 1), 0).astype(F32)
    return own.astype(BF)


def halved(chunks):
    other = 3 - FIRST
    arrived = hop(jnp.stack([chunks[FIRST], chunks[3]]), 2 * FIRST, 0).astype(F32)
    return chunks[0] + arrived[0], chunks[other] + arrived[1]


def shards(inputs, cotangent, expand_w, expand_b, depth_k, depth_b, project_w):
    chan, dp = lax.axis_index("chan"), lax.axis_index("dp")
    pair, zpos = dp & 1, dp >> 1
    groups = lax.axis_size("dp") // 2
    own_rows, ncols, cin = inputs.shape
    nrows = 8 * own_rows
    hslice = expand_w.shape[1]
    half = hslice // 2
    npix = nrows * ncols
    pos = jnp.stack([pair * 4 + chan, pair, zpos, chan & 1]).astype(jnp.int32)

    full = array(nrows, ncols, half)
    mm = vpu = dict(flops=1024, nbytes=1024)
    long = dict(flops=2 * 10**10, nbytes=10**8)
    padded = array(half // LANES, nrows + 4, ncols + 2 * EDGE, LANES, dtype=F32)

    mine = array(*inputs.shape)
    w1, b1, taps, bd, w2, rows_own, cot_own, hidden, grad_pre = kernel(
        prepare_kernel, "prepare",
        (array(cin, half), array(1, half, dtype=F32), array(25, half, dtype=F32), array(1, half, dtype=F32),
         array(half, cin), mine, mine, padded, padded),
        (pos, expand_w, expand_b.reshape(1, hslice), depth_k, depth_b.reshape(1, hslice), project_w, inputs, cotangent),
    )

    def expand(order, into=(), after=(), edges=()):
        return kernel(
            lambda *refs: expand_kernel(order, *refs), "expand%d" % order[0], (padded, full) + edges,
            (pos, w1, b1, *(in_pieces[k] for k in order)), [pltpu.VMEM((own_rows, ncols, half), F32)],
            into=into, after=after, **mm,
        )

    in_pieces = {0: rows_own, 1: hop(inputs, 0, 1)}
    cot_core = hop(cotangent, 0, 1)
    steps = {4: (1, 0), 2: (0, 2), 6: (1, 2)}
    for k, step in steps.items():
        in_pieces[k] = hop(inputs, *step)
    first = expand((0, 1), (hidden,), after=(cot_core,))
    for k in steps:
        in_pieces[k + 1] = hop(tied(in_pieces[k], first[0]), 0, 1)
    second = expand((2, 4), first)
    cot_pair = cross(tied(jnp.stack([cot_own, cot_core]), in_pieces[2], in_pieces[4]), 0)
    cot_far = hop(tied(cotangent, in_pieces[6]), *steps[6])
    in_pieces = [in_pieces[k] for k in range(8)]
    edges = (array(2, ncols, half),) * 2
    hidden, slope_one, *sent = expand((7,), expand((6, 3, 5), second), edges=edges)
    hid_near, hid_far = meet(sent[0], FLIP_HID), meet(sent[1], 1 - FLIP_HID)

    f32_full = array(nrows, ncols, half, dtype=F32)
    inner = kernel(
        lambda *refs: middle_kernel(True, *refs), "inner", (full, f32_full), (pos, taps, bd, hidden), **vpu
    )
    mixed, slope_two, hidden = kernel(
        lambda *refs: middle_kernel(False, *refs), "outer", (full, f32_full, padded),
        (pos, taps, bd, hid_near, hid_far), into=(*inner, hidden), **vpu,
    )
    cot_swap = hop(tied(cot_pair, slope_one), 0, 1)
    cot_last = hop(tied(cot_far, mixed), 0, 1)
    cot_pieces = (cot_own, cot_core, cot_pair, cot_far, cot_swap, cot_last)

    def project(pieces, into=(), after=(), edges=()):
        return kernel(
            lambda *refs: project_kernel(pieces, *refs), "project%d" % pieces[0], (padded,) + edges,
            (pos, w2, slope_two, *(cot_pieces[i] for i in pieces)), into=into, after=after, **mm,
        )

    def chunk_outs(rows, width):
        return (array(rows, width, dtype=F32),) + (array(rows, width),) * (groups - 1)

    half_done = project((0, 1, 2, 3), (grad_pre,))
    w2_chunks = kernel(
        w2_kernel, "w2", chunk_outs(half // groups, cin), (pos, mixed, *cot_pieces),
        [pltpu.VMEM((half, cin), F32)], after=half_done, **mm,
    )
    grad_pre, *sent = project((4, 5), half_done, (w2_chunks[0],), edges)
    gp_near, gp_far = meet(sent[0], FLIP_GP), meet(sent[1], 1 - FLIP_GP)
    tail = 16 * groups
    small = kernel(taps_kernel, "taps", array(tail, half, dtype=F32), (pos, hidden, grad_pre), **vpu)
    four = groups == 4
    w2_halves = halved(w2_chunks) if four else w2_chunks[:1]
    _, grad_act, grad_b1 = kernel(
        back_kernel, "back", (padded, full, array(1, half, dtype=F32)), (pos, taps, gp_near, gp_far, slope_one),
        [pltpu.VMEM((8, LANES), F32)], after=(small, *w2_halves), into=(grad_pre,), **vpu,
    )
    if four:
        w2_sent = hop(tied(w2_halves[1], small).astype(BF), 2 * (3 - FIRST), 0).astype(F32)
        w2_chunk = (tied(w2_halves[0], grad_act) + w2_sent).astype(BF)
    else:
        w2_chunk = summed(tied(w2_chunks[0], grad_act), w2_chunks[1:])
    w2_two = jnp.stack([w2_chunk, hop(w2_chunk, 4, 0)]) if four else None

    block = (own_rows, ncols, cin)
    two = (2, *block)
    to_core = kernel(core_kernel, "core", array(4, *block), (pos, grad_act, w1), after=(w2_chunk,), **mm)
    from_core = hop(to_core, 0, 1)
    w1_own, *w1_sends = kernel(
        w1_kernel, "w1", chunk_outs((cin + tail) // groups, half), (pos, grad_act, small, grad_b1, *in_pieces),
        [pltpu.VMEM((cin + tail, half), F32)], after=(w2_chunk, to_core), **mm,
    )
    going = kernel(
        chip_send_kernel, "chip_send", array(*two), (pos, grad_act, w1, from_core), after=(w1_own,), **mm
    )
    if four:
        w2_far = hop(tied(w2_two, going), 2, 0)
        w2_blocks = [w2_two[0], w2_far[0], w2_two[1], w2_far[1]]
    else:
        w2_blocks = [hop(w2_chunk, 2 * k, 0) if k else w2_chunk for k in range(groups)]
    arrived = cross(going, 0)
    kept = kernel(chip_keep_kernel, "chip_keep", array(*two, dtype=F32), (pos, grad_act, w1, from_core), after=(going,), **mm)
    w1_parts = [hop(send, 2 * (k + 1), 0) for k, send in enumerate(w1_sends)]
    w1_chunk = kernel(sum_kernel, "sum", array(*w1_own.shape), (pos, w1_own, *w1_parts), after=(kept,), **long)
    w1_side = hop(w1_chunk, 1, 0)
    w1_near = [hop(w1_chunk, 2 * k, 0) if k else w1_chunk for k in range(groups)]
    w2_col = kernel(
        column_kernel, "column", array(groups, half // groups + ROOM, cin), (pos, *w2_blocks), after=(w1_chunk,), **mm
    )
    w2_other = hop(w2_col, 1, 0)
    forward = kernel(
        forward_kernel, "forward", array(*block), (pos, kept, arrived), after=(w1_side,), **mm
    )
    onward = cross(forward, 1)
    w1_side = kernel(copy_kernel, "side", array(*w1_side.shape), (pos, w1_side), after=(w1_near[-1],), **long)
    w1_blocks = w1_near + [hop(w1_side, 2 * k, 0) if k else w1_side for k in range(groups)]
    line = array(1, hslice, dtype=F32)
    input_grad, out_w2, out_w1, out_k, out_bd, out_b1 = kernel(
        last_kernel, "last",
        (array(*block), array(hslice, cin, dtype=F32), array(cin, hslice, dtype=F32), array(25, hslice, dtype=F32), line, line),
        (pos, cot_own, kept, arrived, onward, w2_col, w2_other, *w1_blocks),
        [pltpu.VMEM((tail, hslice), F32)],
    )
    return (input_grad, out_w1, out_b1.reshape(hslice), out_k, out_bd.reshape(hslice), out_w2)


def solution(mesh):
    in_specs = (
        P(("dp", "chan"), None, None),
        P(("dp", "chan"), None, None),
        P(None, "chan"),
        P("chan"),
        P(None, "chan"),
        P("chan"),
        P("chan", None),
    )
    out_specs = (
        P(("dp", "chan"), None, None),
        P(None, "chan"),
        P("chan"),
        P(None, "chan"),
        P("chan"),
        P("chan", None),
    )
    return jax.shard_map(shards, mesh=mesh, in_specs=in_specs, out_specs=out_specs, check_vma=False)
```

```python
import jax
import jax.numpy as jnp
from jax import lax
from jax.experimental import pallas as pl
from jax.experimental.pallas import tpu as pltpu
from jax.sharding import PartitionSpec as P

BF = jnp.bfloat16
F32 = jnp.float32
AXES = ("dp", "chan")
VMEM = pl.BlockSpec(memory_space=pltpu.VMEM)
SMEM = pl.BlockSpec(memory_space=pltpu.SMEM)
ANY = pl.BlockSpec(memory_space=pl.ANY)
EDGE = 8
LANES = 128
FLIP_HID, FLIP_GP = 0, 1
FIRST = 2
ROOM = 0


def array(*shape, dtype=BF):
    return jax.ShapeDtypeStruct(shape, dtype)


def kernel(body, name, out, args, scratch=(), flops=0, nbytes=0, after=(), into=()):
    first, last = len(args), len(args) + len(after) + len(into)

    def run(*refs):
        body(*refs[:first], *refs[last:])

    return pl.pallas_call(
        run,
        out_shape=out,
        in_specs=[SMEM] + [VMEM] * (len(args) - 1) + [ANY] * len(after) + [VMEM] * len(into),
        out_specs=jax.tree.map(lambda _: VMEM, out),
        scratch_shapes=list(scratch),
        compiler_params=pltpu.CompilerParams(vmem_limit_bytes=16 * 1024 * 1024),
        cost_estimate=pl.CostEstimate(flops=flops, bytes_accessed=nbytes, transcendentals=0),
        input_output_aliases={len(args) + len(after) + i: i for i in range(len(into))},
        name=name,
    )(*args, *after, *into)


def gelu_parts(pre):
    cdf = 0.5 * (1.0 + lax.erf(pre * 0.7071067811865476))
    dens = jnp.exp(-0.5 * pre * pre) * 0.3989422804014327
    return pre * cdf, cdf + pre * dens


def hop(value, dp_xor, chan_xor):
    ndp, nchan = lax.axis_size("dp"), lax.axis_size("chan")
    pairs = [
        (d * nchan + c, (d ^ dp_xor) * nchan + (c ^ chan_xor))
        for d in range(ndp)
        for c in range(nchan)
    ]
    return lax.ppermute(value, AXES, pairs)


def cross(value, turn):
    ndp, nchan = lax.axis_size("dp"), lax.axis_size("chan")
    pairs = []
    for d in range(ndp):
        for c in range(nchan):
            to = (d ^ 1, c) if (c & 1) == turn else (d, c ^ 2)
            pairs.append((d * nchan + c, to[0] * nchan + to[1]))
    return lax.ppermute(value, AXES, pairs)


def meet(value, odd):
    ndp, nchan = lax.axis_size("dp"), lax.axis_size("chan")
    pairs = []
    for d in range(ndp):
        to = d + 2 if (d // 2) % 2 == odd else d - 2
        if 0 <= to < ndp:
            pairs += [(d * nchan + c, to * nchan + c) for c in range(nchan)]
    return lax.ppermute(value, AXES, pairs)


def tied(value, *others):
    return lax.optimization_barrier((value, *others))[0]


def prepare_kernel(pos, w1, b1, taps, b2, w2, rows, cot, w1_own, b1_own, taps_own, b2_own, w2_own, rows_own, cot_own, *pads):
    half = b1_own.shape[1]
    cut = pl.ds(pl.multiple_of(pos[1] * half, half), half)
    w1_own[...] = w1[:, cut]
    b1_own[...] = b1[:, cut]
    taps_own[...] = taps[:, cut]
    b2_own[...] = b2[:, cut]
    w2_own[...] = w2[cut, :]
    rows_own[...] = rows[...]
    cot_own[...] = cot[...]
    for pad in pads:
        zeros = jnp.zeros((pad.shape[0], pad.shape[1], EDGE, LANES), F32)
        pad[:, :, 0:EDGE, :] = zeros
        pad[:, :, pad.shape[2] - EDGE :, :] = zeros


def cuts(half):
    return [(c, slice(c * LANES, (c + 1) * LANES)) for c in range(half // LANES)]


def put_rows(pad, at, value):
    rows, ncols, half = value.shape
    value = value.astype(BF).astype(F32)
    for c, cut in cuts(half):
        pad[c, pl.ds(at + 2, rows), EDGE : EDGE + ncols, :] = value[:, :, cut]


def put_edges(pos, pad, edges, flip):
    _, ncols, half = edges[0].shape
    last = pad.shape[1] - 6
    odd = (pos[2] & 1) ^ flip
    for edge, at in zip(edges, (last * (1 - odd), last * odd)):
        for c, cut in cuts(half):
            edge[:, :, cut] = pad[c, pl.ds(at + 2, 2), EDGE : EDGE + ncols, :].astype(BF)


def put_halo(pos, pad, near, far, flip):
    _, ncols, half = near.shape
    last = pad.shape[1] - 2
    odd = (pos[2] & 1) ^ flip
    for edge, at in zip((near, far), (last * (1 - odd), last * odd)):
        for c, cut in cuts(half):
            pad[c, pl.ds(at, 2), EDGE : EDGE + ncols, :] = edge[:, :, cut].astype(F32)


def expand_kernel(order, pos, w, b, *refs):
    pieces, (hid, slope, *edges, pre) = refs[: len(order)], refs[len(order) :]
    n, ncols, cin = pieces[0].shape
    half = slope.shape[2]
    for k, piece in zip(order, pieces):
        at = (pos[0] ^ k) * n
        pre[...] = (
            jnp.dot(piece[...].reshape(n * ncols, cin), w[...], preferred_element_type=F32) + b[...]
        ).reshape(n, ncols, half)

        def body(r, carry, at=at):
            h, s = gelu_parts(pre[pl.ds(r, 1)])
            put_rows(hid, at + r, h)
            slope[pl.ds(at + r, 1)] = s.astype(BF)
            return carry

        lax.fori_loop(0, n, body, 0)
    if edges:
        put_edges(pos, hid, edges, FLIP_HID)


def conv_tiles(pad, taps, cut, ncols, starts, nr, cols, flip, emit):
    def body(i, carry):
        w0 = i * cols
        for r0 in starts:
            acc = [None] * nr
            for j in range(5):
                xs = [pad[r0 + q, pl.ds(w0 + (EDGE - 2) + j, cols), :] for q in range(nr + 4)]
                for q in range(5):
                    t = 5 * q + j
                    t = 24 - t if flip else t
                    for r in range(nr):
                        term = taps[t : t + 1, cut] * xs[r + q]
                        acc[r] = term if acc[r] is None else acc[r] + term
            emit(r0, pl.ds(pl.multiple_of(w0, cols), cols), acc)
        return carry

    lax.fori_loop(0, ncols // cols, body, 0)


def middle_kernel(inner, pos, taps, bias, *refs):
    if inner:
        pad, mixed, slope = refs
    else:
        near, far, mixed, slope, pad = refs
        put_halo(pos, pad, near, far, FLIP_HID)
    nrows, ncols, half = mixed.shape
    for c, cut in cuts(half):
        add = bias[:, cut]

        def emit(r0, w, acc, cut=cut, add=add):
            for r in range(len(acc)):
                m, s = gelu_parts(acc[r] + add)
                mixed[r0 + r, w, cut] = m.astype(BF)
                slope[r0 + r, w, cut] = s

        if inner:
            conv_tiles(pad.at[c], taps, cut, ncols, range(2, nrows - 2, 4), 4, 16, False, emit)
        else:
            conv_tiles(pad.at[c], taps, cut, ncols, (0, nrows - 2), 2, 32, False, emit)


def cot_blocks(pos, which, refs):
    core = pos[3]
    found = []
    for i, ref in zip(which, refs):
        if i in (2, 4):
            found += [((4 - 2 * core if i == 2 else 3 + 2 * core) + (j if i == 2 else -j), ref.at[j]) for j in range(2)]
        else:
            found.append(({0: 0, 1: 1, 3: 6, 5: 7}[i], ref))
    return found


def project_kernel(which, pos, weights, slope, *refs):
    pieces, (gp, *edges) = cot_blocks(pos, which, refs[: len(which)]), refs[len(which) :]
    n, ncols, cin = pieces[0][1].shape
    half = slope.shape[2]
    for k, piece in pieces:
        at = (pos[0] ^ k) * n
        res = lax.dot_general(
            piece[...].reshape(n * ncols, cin), weights[...], (((1,), (1,)), ((), ())), preferred_element_type=F32
        )
        put_rows(gp, at, res.reshape(n, ncols, half) * slope[pl.ds(at, n)])
    if edges:
        put_edges(pos, gp, edges, FLIP_GP)


def outer_sum(pos, total, pieces, values, swap):
    n, ncols, _ = pieces[0][1].shape
    for i, (k, piece) in enumerate(pieces):
        a = piece[...].reshape(n * ncols, -1)
        b = values[pl.ds((pos[0] ^ k) * n, n)].reshape(n * ncols, -1)
        if swap:
            a, b = b, a
        part = lax.dot_general(a, b, (((0,), (0,)), ((), ())), preferred_element_type=F32)
        if i == 0:
            total[0 : part.shape[0], :] = part
        else:
            total[0 : part.shape[0], :] += part


def w2_kernel(pos, mixed, *refs):
    pieces, outs, total = cot_blocks(pos, range(6), refs[:6]), refs[6:-1], refs[-1]
    outer_sum(pos, total, pieces, mixed, True)
    n = outs[0].shape[0]
    for k, ref in enumerate(outs):
        ref[...] = total[pl.ds(pl.multiple_of((pos[2] ^ k) * n, n), n), :].astype(ref.dtype)


def taps_kernel(pos, hid, gp, small):
    _, nrows, ncols, _ = hid.shape
    nrows, ncols = nrows - 4, ncols - 2 * EDGE
    small[...] = jnp.zeros_like(small)
    for c, cut in cuts(small.shape[1]):

        def body(i, accs, c=c):
            accs = list(accs)
            w0 = i * 8
            for j in range(5):
                xs = [hid[c, q, pl.ds(w0 + (EDGE - 2) + j, 8), :] for q in range(4)]
                for r in range(nrows):
                    xs.append(hid[c, r + 4, pl.ds(w0 + (EDGE - 2) + j, 8), :])
                    g = gp[c, r + 2, pl.ds(pl.multiple_of(w0 + EDGE, 8), 8), :]
                    for q in range(5):
                        accs[5 * q + j] = accs[5 * q + j] + xs[r + q] * g
                    if j == 0:
                        accs[25] = accs[25] + g
            return tuple(accs)

        zero = jnp.zeros((8, LANES), F32)
        accs = lax.fori_loop(0, ncols // 8, body, (zero,) * 26)
        for t in range(26):
            small[t : t + 1, cut] = jnp.sum(accs[t], axis=0, keepdims=True)


def back_kernel(pos, taps, near, far, slope, pad, act, grad_b, total):
    nrows, ncols, half = act.shape
    put_halo(pos, pad, near, far, FLIP_GP)
    for c, cut in cuts(half):
        total[...] = jnp.zeros_like(total)

        def emit(r0, w, acc, cut=cut):
            part = jnp.zeros((8, LANES), F32)
            for r in range(4):
                a = (acc[r] * slope[r0 + r, w, cut].astype(F32)).astype(BF)
                act[r0 + r, w, cut] = a
                part = part + jnp.sum(a.astype(F32).reshape(-1, 8, LANES), axis=0)
            total[...] += part

        conv_tiles(pad.at[c], taps, cut, ncols, range(0, nrows, 4), 4, 16, True, emit)
        grad_b[:, cut] = jnp.sum(total[...], axis=0, keepdims=True)


def w1_kernel(pos, act, small, grad_b, *refs):
    pieces, outs, total = refs[:8], refs[8:-1], refs[-1]
    outer_sum(pos, total, list(enumerate(pieces)), act, False)
    cin = pieces[0].shape[2]
    total[cin:, :] = small[...]
    total[cin + 26 : cin + 27, :] = grad_b[...]
    chunks = len(outs)
    n, m = cin // chunks, small.shape[0] // chunks
    for k, ref in enumerate(outs):
        at = pos[2] ^ k
        ref[0:n, :] = total[pl.ds(pl.multiple_of(at * n, n), n), :].astype(ref.dtype)
        ref[n:, :] = total[pl.ds(pl.multiple_of(cin + at * m, m), m), :].astype(ref.dtype)


def share(pos, act, w, chip_xor, core):
    ncols, half = act.shape[1:]
    n = act.shape[0] // 8
    at = (((pos[0] // 2) ^ chip_xor) * 2 + core) * n
    return lax.dot_general(
        act[pl.ds(at, n)].reshape(n * ncols, half), w[...], (((1,), (1,)), ((), ())), preferred_element_type=F32
    ).reshape(n, ncols, -1)


def core_kernel(pos, act, w, out):
    for k in range(4):
        out[k] = share(pos, act, w, k, 1 - pos[3]).astype(BF)


def chip_send_kernel(pos, act, w, other, out):
    for i, k in enumerate((2 - pos[3], 3)):
        out[i] = (share(pos, act, w, k, pos[3]) + other[k].astype(F32)).astype(BF)


def chip_keep_kernel(pos, act, w, other, out):
    for i, k in enumerate((0, 1 + pos[3])):
        out[i] = share(pos, act, w, k, pos[3]) + other[k].astype(F32)


def forward_kernel(pos, kept, arrived, out):
    out[...] = (kept[1] + arrived[1].astype(F32)).astype(BF)


def finish_kernel(pos, cot, kept, arrived, last, out):
    out[...] = (cot[...].astype(F32) + (kept[0] + arrived[0].astype(F32) + last[...].astype(F32))).astype(BF)


def sum_kernel(pos, own, *refs):
    total = own[...]
    for part in refs[:-1]:
        total = total + part[...].astype(F32)
    refs[-1][...] = total.astype(BF)


def copy_kernel(pos, value, out):
    out[...] = value[...]


def column_kernel(pos, *refs):
    blocks, out = refs[:-1], refs[-1]
    n = blocks[0].shape[0]
    for k, block in enumerate(blocks):
        out[pos[2] ^ k, 0:n] = block[...]
        if n < out.shape[1]:
            out[pos[2] ^ k, n:] = jnp.zeros((out.shape[1] - n, out.shape[2]), out.dtype)


def w2_place_kernel(pos, mine, other, out):
    g, _, cin = mine.shape
    n = out.shape[0] // (2 * g)
    for k, col in enumerate((mine, other)):
        for i in range(g):
            out[pl.ds(pl.multiple_of(((pos[1] ^ k) * g + i) * n, n), n), :] = col[i, 0:n].astype(F32)


def w1_place_kernel(pos, blocks, out, grad_k, grad_bd, grad_b1, small):
    g = len(blocks) // 2
    half = blocks[0].shape[1]
    n = out.shape[0] // g
    m = small.shape[0] // g
    for i, block in enumerate(blocks):
        cut = pl.ds(pl.multiple_of((pos[1] ^ (i // g)) * half, half), half)
        at = pos[2] ^ (i % g)
        out[pl.ds(pl.multiple_of(at * n, n), n), cut] = block[0:n, :].astype(F32)
        small[pl.ds(pl.multiple_of(at * m, m), m), cut] = block[n:, :].astype(F32)
    grad_k[...] = small[0:25, :]
    grad_bd[...] = small[25:26, :]
    grad_b1[...] = small[26:27, :]


def last_kernel(pos, cot, kept, arrived, last, mine, other, *refs):
    blocks, (out, out_w2, out_w1, grad_k, grad_bd, grad_b1, small) = refs[:-7], refs[-7:]
    finish_kernel(pos, cot, kept, arrived, last, out)
    w2_place_kernel(pos, mine, other, out_w2)
    w1_place_kernel(pos, blocks, out_w1, grad_k, grad_bd, grad_b1, small)


def summed(own, sends):
    for k, send in enumerate(sends):
        own = own + hop(send, 2 * (k + 1), 0).astype(F32)
    return own.astype(BF)


def halved(chunks):
    other = 3 - FIRST
    arrived = hop(jnp.stack([chunks[FIRST], chunks[3]]), 2 * FIRST, 0).astype(F32)
    return chunks[0] + arrived[0], chunks[other] + arrived[1]


def shards(inputs, cotangent, expand_w, expand_b, depth_k, depth_b, project_w):
    chan, dp = lax.axis_index("chan"), lax.axis_index("dp")
    pair, zpos = dp & 1, dp >> 1
    groups = lax.axis_size("dp") // 2
    own_rows, ncols, cin = inputs.shape
    nrows = 8 * own_rows
    hslice = expand_w.shape[1]
    half = hslice // 2
    npix = nrows * ncols
    pos = jnp.stack([pair * 4 + chan, pair, zpos, chan & 1]).astype(jnp.int32)

    full = array(nrows, ncols, half)
    mm = vpu = dict(flops=1024, nbytes=1024)
    long = dict(flops=2 * 10**10, nbytes=10**8)
    padded = array(half // LANES, nrows + 4, ncols + 2 * EDGE, LANES, dtype=F32)

    mine = array(*inputs.shape)
    w1, b1, taps, bd, w2, rows_own, cot_own, hidden, grad_pre = kernel(
        prepare_kernel, "prepare",
        (array(cin, half), array(1, half, dtype=F32), array(25, half, dtype=F32), array(1, half, dtype=F32),
         array(half, cin), mine, mine, padded, padded),
        (pos, expand_w, expand_b.reshape(1, hslice), depth_k, depth_b.reshape(1, hslice), project_w, inputs, cotangent),
    )

    def expand(order, into=(), after=(), edges=()):
        return kernel(
            lambda *refs: expand_kernel(order, *refs), "expand%d" % order[0], (padded, full) + edges,
            (pos, w1, b1, *(in_pieces[k] for k in order)), [pltpu.VMEM((own_rows, ncols, half), F32)],
            into=into, after=after, **mm,
        )

    in_pieces = {0: rows_own, 1: hop(inputs, 0, 1)}
    cot_core = hop(cotangent, 0, 1)
    steps = {4: (1, 0), 2: (0, 2), 6: (1, 2)}
    for k, step in steps.items():
        in_pieces[k] = hop(inputs, *step)
    first = expand((0, 1), (hidden,), after=(cot_core,))
    for k in steps:
        in_pieces[k + 1] = hop(tied(in_pieces[k], first[0]), 0, 1)
    second = expand((2, 4), first)
    cot_pair = cross(tied(jnp.stack([cot_own, cot_core]), in_pieces[2], in_pieces[4]), 0)
    cot_far = hop(tied(cotangent, in_pieces[6]), *steps[6])
    in_pieces = [in_pieces[k] for k in range(8)]
    edges = (array(2, ncols, half),) * 2
    hidden, slope_one, *sent = expand((7,), expand((6, 3, 5), second), edges=edges)
    hid_near, hid_far = meet(sent[0], FLIP_HID), meet(sent[1], 1 - FLIP_HID)

    f32_full = array(nrows, ncols, half, dtype=F32)
    inner = kernel(
        lambda *refs: middle_kernel(True, *refs), "inner", (full, f32_full), (pos, taps, bd, hidden), **long
    )
    mixed, slope_two, hidden = kernel(
        lambda *refs: middle_kernel(False, *refs), "outer", (full, f32_full, padded),
        (pos, taps, bd, hid_near, hid_far), into=(*inner, hidden), **vpu,
    )
    cot_swap = hop(tied(cot_pair, slope_one), 0, 1)
    cot_last = hop(tied(cot_far, mixed), 0, 1)
    cot_pieces = (cot_own, cot_core, cot_pair, cot_far, cot_swap, cot_last)

    def project(pieces, into=(), after=(), edges=()):
        return kernel(
            lambda *refs: project_kernel(pieces, *refs), "project%d" % pieces[0], (padded,) + edges,
            (pos, w2, slope_two, *(cot_pieces[i] for i in pieces)), into=into, after=after, **mm,
        )

    def chunk_outs(rows, width):
        return (array(rows, width, dtype=F32),) + (array(rows, width),) * (groups - 1)

    half_done = project((0, 1, 2, 3), (grad_pre,))
    w2_chunks = kernel(
        w2_kernel, "w2", chunk_outs(half // groups, cin), (pos, mixed, *cot_pieces),
        [pltpu.VMEM((half, cin), F32)], after=half_done, **mm,
    )
    grad_pre, *sent = project((4, 5), half_done, (w2_chunks[0],), edges)
    gp_near, gp_far = meet(sent[0], FLIP_GP), meet(sent[1], 1 - FLIP_GP)
    tail = 16 * groups
    small = kernel(taps_kernel, "taps", array(tail, half, dtype=F32), (pos, hidden, grad_pre), **vpu)
    four = groups == 4
    w2_halves = halved(w2_chunks) if four else w2_chunks[:1]
    _, grad_act, grad_b1 = kernel(
        back_kernel, "back", (padded, full, array(1, half, dtype=F32)), (pos, taps, gp_near, gp_far, slope_one),
        [pltpu.VMEM((8, LANES), F32)], after=(small, *w2_halves), into=(grad_pre,), **vpu,
    )
    if four:
        w2_sent = hop(tied(w2_halves[1], small).astype(BF), 2 * (3 - FIRST), 0).astype(F32)
        w2_chunk = (tied(w2_halves[0], grad_act) + w2_sent).astype(BF)
    else:
        w2_chunk = summed(tied(w2_chunks[0], grad_act), w2_chunks[1:])
    w2_two = jnp.stack([w2_chunk, hop(w2_chunk, 4, 0)]) if four else None

    block = (own_rows, ncols, cin)
    two = (2, *block)
    to_core = kernel(core_kernel, "core", array(4, *block), (pos, grad_act, w1), after=(w2_chunk,), **mm)
    from_core = hop(to_core, 0, 1)
    w1_own, *w1_sends = kernel(
        w1_kernel, "w1", chunk_outs((cin + tail) // groups, half), (pos, grad_act, small, grad_b1, *in_pieces),
        [pltpu.VMEM((cin + tail, half), F32)], after=(w2_chunk, to_core), **mm,
    )
    going = kernel(
        chip_send_kernel, "chip_send", array(*two), (pos, grad_act, w1, from_core), after=(w1_own,), **mm
    )
    if four:
        w2_far = hop(tied(w2_two, going), 2, 0)
        w2_blocks = [w2_two[0], w2_far[0], w2_two[1], w2_far[1]]
    else:
        w2_blocks = [hop(w2_chunk, 2 * k, 0) if k else w2_chunk for k in range(groups)]
    arrived = cross(going, 0)
    kept = kernel(chip_keep_kernel, "chip_keep", array(*two, dtype=F32), (pos, grad_act, w1, from_core), after=(going,), **mm)
    w1_parts = [hop(send, 2 * (k + 1), 0) for k, send in enumerate(w1_sends)]
    w1_chunk = kernel(sum_kernel, "sum", array(*w1_own.shape), (pos, w1_own, *w1_parts), after=(kept,), **long)
    w1_side = hop(w1_chunk, 1, 0)
    w1_near = [hop(w1_chunk, 2 * k, 0) if k else w1_chunk for k in range(groups)]
    w2_col = kernel(
        column_kernel, "column", array(groups, half // groups + ROOM, cin), (pos, *w2_blocks), after=(w1_chunk,), **mm
    )
    w2_other = hop(w2_col, 1, 0)
    forward = kernel(
        forward_kernel, "forward", array(*block), (pos, kept, arrived), after=(w1_side,), **mm
    )
    onward = cross(forward, 1)
    w1_side = kernel(copy_kernel, "side", array(*w1_side.shape), (pos, w1_side), after=(w1_near[-1],), **long)
    w1_blocks = w1_near + [hop(w1_side, 2 * k, 0) if k else w1_side for k in range(groups)]
    line = array(1, hslice, dtype=F32)
    input_grad, out_w2, out_w1, out_k, out_bd, out_b1 = kernel(
        last_kernel, "last",
        (array(*block), array(hslice, cin, dtype=F32), array(cin, hslice, dtype=F32), array(25, hslice, dtype=F32), line, line),
        (pos, cot_own, kept, arrived, onward, w2_col, w2_other, *w1_blocks),
        [pltpu.VMEM((tail, hslice), F32)],
    )
    return (input_grad, out_w1, out_b1.reshape(hslice), out_k, out_bd.reshape(hslice), out_w2)


def solution(mesh):
    in_specs = (
        P(("dp", "chan"), None, None),
        P(("dp", "chan"), None, None),
        P(None, "chan"),
        P("chan"),
        P(None, "chan"),
        P("chan"),
        P("chan", None),
    )
    out_specs = (
        P(("dp", "chan"), None, None),
        P(None, "chan"),
        P("chan"),
        P(None, "chan"),
        P("chan"),
        P("chan", None),
    )
    return jax.shard_map(shards, mesh=mesh, in_specs=in_specs, out_specs=out_specs, check_vma=False)
```

```python
import jax
import jax.numpy as jnp
from jax import lax
from jax.experimental import pallas as pl
from jax.experimental.pallas import tpu as pltpu
from jax.sharding import PartitionSpec as P

BF = jnp.bfloat16
F32 = jnp.float32
AXES = ("dp", "chan")
VMEM = pl.BlockSpec(memory_space=pltpu.VMEM)
SMEM = pl.BlockSpec(memory_space=pltpu.SMEM)
ANY = pl.BlockSpec(memory_space=pl.ANY)
EDGE = 8
LANES = 128
FLIP_HID, FLIP_GP = 0, 1
FIRST = 2
ROOM = 0


def array(*shape, dtype=BF):
    return jax.ShapeDtypeStruct(shape, dtype)


def kernel(body, name, out, args, scratch=(), flops=0, nbytes=0, after=(), into=()):
    first, last = len(args), len(args) + len(after) + len(into)

    def run(*refs):
        body(*refs[:first], *refs[last:])

    return pl.pallas_call(
        run,
        out_shape=out,
        in_specs=[SMEM] + [VMEM] * (len(args) - 1) + [ANY] * len(after) + [VMEM] * len(into),
        out_specs=jax.tree.map(lambda _: VMEM, out),
        scratch_shapes=list(scratch),
        compiler_params=pltpu.CompilerParams(vmem_limit_bytes=16 * 1024 * 1024),
        cost_estimate=pl.CostEstimate(flops=flops, bytes_accessed=nbytes, transcendentals=0),
        input_output_aliases={len(args) + len(after) + i: i for i in range(len(into))},
        name=name,
    )(*args, *after, *into)


def gelu_parts(pre):
    cdf = 0.5 * (1.0 + lax.erf(pre * 0.7071067811865476))
    dens = jnp.exp(-0.5 * pre * pre) * 0.3989422804014327
    return pre * cdf, cdf + pre * dens


def hop(value, dp_xor, chan_xor):
    ndp, nchan = lax.axis_size("dp"), lax.axis_size("chan")
    pairs = [
        (d * nchan + c, (d ^ dp_xor) * nchan + (c ^ chan_xor))
        for d in range(ndp)
        for c in range(nchan)
    ]
    return lax.ppermute(value, AXES, pairs)


def cross(value, turn):
    ndp, nchan = lax.axis_size("dp"), lax.axis_size("chan")
    pairs = []
    for d in range(ndp):
        for c in range(nchan):
            to = (d ^ 1, c) if (c & 1) == turn else (d, c ^ 2)
            pairs.append((d * nchan + c, to[0] * nchan + to[1]))
    return lax.ppermute(value, AXES, pairs)


def meet(value, odd):
    ndp, nchan = lax.axis_size("dp"), lax.axis_size("chan")
    pairs = []
    for d in range(ndp):
        to = d + 2 if (d // 2) % 2 == odd else d - 2
        if 0 <= to < ndp:
            pairs += [(d * nchan + c, to * nchan + c) for c in range(nchan)]
    return lax.ppermute(value, AXES, pairs)


def tied(value, *others):
    return lax.optimization_barrier((value, *others))[0]


def prepare_kernel(pos, w1, b1, taps, b2, w2, rows, cot, w1_own, b1_own, taps_own, b2_own, w2_own, rows_own, cot_own, *pads):
    half = b1_own.shape[1]
    cut = pl.ds(pl.multiple_of(pos[1] * half, half), half)
    w1_own[...] = w1[:, cut]
    b1_own[...] = b1[:, cut]
    taps_own[...] = taps[:, cut]
    b2_own[...] = b2[:, cut]
    w2_own[...] = w2[cut, :]
    rows_own[...] = rows[...]
    cot_own[...] = cot[...]
    for pad in pads:
        zeros = jnp.zeros((pad.shape[0], pad.shape[1], EDGE, LANES), F32)
        pad[:, :, 0:EDGE, :] = zeros
        pad[:, :, pad.shape[2] - EDGE :, :] = zeros


def cuts(half):
    return [(c, slice(c * LANES, (c + 1) * LANES)) for c in range(half // LANES)]


def put_rows(pad, at, value):
    rows, ncols, half = value.shape
    value = value.astype(BF).astype(F32)
    for c, cut in cuts(half):
        pad[c, pl.ds(at + 2, rows), EDGE : EDGE + ncols, :] = value[:, :, cut]


def put_edges(pos, pad, edges, flip):
    _, ncols, half = edges[0].shape
    last = pad.shape[1] - 6
    odd = (pos[2] & 1) ^ flip
    for edge, at in zip(edges, (last * (1 - odd), last * odd)):
        for c, cut in cuts(half):
            edge[:, :, cut] = pad[c, pl.ds(at + 2, 2), EDGE : EDGE + ncols, :].astype(BF)


def put_halo(pos, pad, near, far, flip):
    _, ncols, half = near.shape
    last = pad.shape[1] - 2
    odd = (pos[2] & 1) ^ flip
    for edge, at in zip((near, far), (last * (1 - odd), last * odd)):
        for c, cut in cuts(half):
            pad[c, pl.ds(at, 2), EDGE : EDGE + ncols, :] = edge[:, :, cut].astype(F32)


def expand_kernel(order, pos, w, b, *refs):
    pieces, (hid, slope, *edges, pre) = refs[: len(order)], refs[len(order) :]
    n, ncols, cin = pieces[0].shape
    half = slope.shape[2]
    for k, piece in zip(order, pieces):
        at = (pos[0] ^ k) * n
        pre[...] = (
            jnp.dot(piece[...].reshape(n * ncols, cin), w[...], preferred_element_type=F32) + b[...]
        ).reshape(n, ncols, half)

        def body(r, carry, at=at):
            h, s = gelu_parts(pre[pl.ds(r, 1)])
            put_rows(hid, at + r, h)
            slope[pl.ds(at + r, 1)] = s.astype(BF)
            return carry

        lax.fori_loop(0, n, body, 0)
    if edges:
        put_edges(pos, hid, edges, FLIP_HID)


def conv_tiles(pad, taps, cut, ncols, starts, nr, cols, flip, emit):
    def body(i, carry):
        w0 = i * cols
        for r0 in starts:
            acc = [None] * nr
            for j in range(5):
                xs = [pad[r0 + q, pl.ds(w0 + (EDGE - 2) + j, cols), :] for q in range(nr + 4)]
                for q in range(5):
                    t = 5 * q + j
                    t = 24 - t if flip else t
                    for r in range(nr):
                        term = taps[t : t + 1, cut] * xs[r + q]
                        acc[r] = term if acc[r] is None else acc[r] + term
            emit(r0, pl.ds(pl.multiple_of(w0, cols), cols), acc)
        return carry

    lax.fori_loop(0, ncols // cols, body, 0)


def middle_kernel(inner, pos, taps, bias, *refs):
    if inner:
        pad, mixed, slope = refs
    else:
        near, far, mixed, slope, pad = refs
        put_halo(pos, pad, near, far, FLIP_HID)
    nrows, ncols, half = mixed.shape
    for c, cut in cuts(half):
        add = bias[:, cut]

        def emit(r0, w, acc, cut=cut, add=add):
            for r in range(len(acc)):
                m, s = gelu_parts(acc[r] + add)
                mixed[r0 + r, w, cut] = m.astype(BF)
                slope[r0 + r, w, cut] = s

        if inner:
            conv_tiles(pad.at[c], taps, cut, ncols, range(2, nrows - 2, 4), 4, 16, False, emit)
        else:
            conv_tiles(pad.at[c], taps, cut, ncols, (0, nrows - 2), 2, 32, False, emit)


def cot_blocks(pos, which, refs):
    core = pos[3]
    found = []
    for i, ref in zip(which, refs):
        if i in (2, 4):
            found += [((4 - 2 * core if i == 2 else 3 + 2 * core) + (j if i == 2 else -j), ref.at[j]) for j in range(2)]
        else:
            found.append(({0: 0, 1: 1, 3: 6, 5: 7}[i], ref))
    return found


def project_kernel(which, pos, weights, slope, *refs):
    pieces, (gp, *edges) = cot_blocks(pos, which, refs[: len(which)]), refs[len(which) :]
    n, ncols, cin = pieces[0][1].shape
    half = slope.shape[2]
    for k, piece in pieces:
        at = (pos[0] ^ k) * n
        res = lax.dot_general(
            piece[...].reshape(n * ncols, cin), weights[...], (((1,), (1,)), ((), ())), preferred_element_type=F32
        )
        put_rows(gp, at, res.reshape(n, ncols, half) * slope[pl.ds(at, n)])
    if edges:
        put_edges(pos, gp, edges, FLIP_GP)


def outer_sum(pos, total, pieces, values, swap):
    n, ncols, _ = pieces[0][1].shape
    for i, (k, piece) in enumerate(pieces):
        a = piece[...].reshape(n * ncols, -1)
        b = values[pl.ds((pos[0] ^ k) * n, n)].reshape(n * ncols, -1)
        if swap:
            a, b = b, a
        part = lax.dot_general(a, b, (((0,), (0,)), ((), ())), preferred_element_type=F32)
        if i == 0:
            total[0 : part.shape[0], :] = part
        else:
            total[0 : part.shape[0], :] += part


def w2_kernel(pos, mixed, *refs):
    pieces, outs, total = cot_blocks(pos, range(6), refs[:6]), refs[6:-1], refs[-1]
    outer_sum(pos, total, pieces, mixed, True)
    n = outs[0].shape[0]
    for k, ref in enumerate(outs):
        ref[...] = total[pl.ds(pl.multiple_of((pos[2] ^ k) * n, n), n), :].astype(ref.dtype)


def taps_kernel(pos, hid, gp, small):
    _, nrows, ncols, _ = hid.shape
    nrows, ncols = nrows - 4, ncols - 2 * EDGE
    small[...] = jnp.zeros_like(small)
    for c, cut in cuts(small.shape[1]):

        def body(i, accs, c=c):
            accs = list(accs)
            w0 = i * 8
            for j in range(5):
                xs = [hid[c, q, pl.ds(w0 + (EDGE - 2) + j, 8), :] for q in range(4)]
                for r in range(nrows):
                    xs.append(hid[c, r + 4, pl.ds(w0 + (EDGE - 2) + j, 8), :])
                    g = gp[c, r + 2, pl.ds(pl.multiple_of(w0 + EDGE, 8), 8), :]
                    for q in range(5):
                        accs[5 * q + j] = accs[5 * q + j] + xs[r + q] * g
                    if j == 0:
                        accs[25] = accs[25] + g
            return tuple(accs)

        zero = jnp.zeros((8, LANES), F32)
        accs = lax.fori_loop(0, ncols // 8, body, (zero,) * 26)
        for t in range(26):
            small[t : t + 1, cut] = jnp.sum(accs[t], axis=0, keepdims=True)


def back_kernel(pos, taps, near, far, slope, pad, act, grad_b, total):
    nrows, ncols, half = act.shape
    put_halo(pos, pad, near, far, FLIP_GP)
    for c, cut in cuts(half):
        total[...] = jnp.zeros_like(total)

        def emit(r0, w, acc, cut=cut):
            part = jnp.zeros((8, LANES), F32)
            for r in range(4):
                a = (acc[r] * slope[r0 + r, w, cut].astype(F32)).astype(BF)
                act[r0 + r, w, cut] = a
                part = part + jnp.sum(a.astype(F32).reshape(-1, 8, LANES), axis=0)
            total[...] += part

        conv_tiles(pad.at[c], taps, cut, ncols, range(0, nrows, 4), 4, 16, True, emit)
        grad_b[:, cut] = jnp.sum(total[...], axis=0, keepdims=True)


def w1_kernel(pos, act, small, grad_b, *refs):
    pieces, outs, total = refs[:8], refs[8:-1], refs[-1]
    outer_sum(pos, total, list(enumerate(pieces)), act, False)
    cin = pieces[0].shape[2]
    total[cin:, :] = small[...]
    total[cin + 26 : cin + 27, :] = grad_b[...]
    chunks = len(outs)
    n, m = cin // chunks, small.shape[0] // chunks
    for k, ref in enumerate(outs):
        at = pos[2] ^ k
        ref[0:n, :] = total[pl.ds(pl.multiple_of(at * n, n), n), :].astype(ref.dtype)
        ref[n:, :] = total[pl.ds(pl.multiple_of(cin + at * m, m), m), :].astype(ref.dtype)


def share(pos, act, w, chip_xor, core):
    ncols, half = act.shape[1:]
    n = act.shape[0] // 8
    at = (((pos[0] // 2) ^ chip_xor) * 2 + core) * n
    return lax.dot_general(
        act[pl.ds(at, n)].reshape(n * ncols, half), w[...], (((1,), (1,)), ((), ())), preferred_element_type=F32
    ).reshape(n, ncols, -1)


def core_kernel(pos, act, w, out):
    for k in range(4):
        out[k] = share(pos, act, w, k, 1 - pos[3]).astype(BF)


def chip_send_kernel(pos, act, w, other, out):
    for i, k in enumerate((2 - pos[3], 3)):
        out[i] = (share(pos, act, w, k, pos[3]) + other[k].astype(F32)).astype(BF)


def chip_keep_kernel(pos, act, w, other, out):
    for i, k in enumerate((0, 1 + pos[3])):
        out[i] = share(pos, act, w, k, pos[3]) + other[k].astype(F32)


def forward_kernel(pos, kept, arrived, out):
    out[...] = (kept[1] + arrived[1].astype(F32)).astype(BF)


def finish_kernel(pos, cot, kept, arrived, last, out):
    out[...] = (cot[...].astype(F32) + (kept[0] + arrived[0].astype(F32) + last[...].astype(F32))).astype(BF)


def sum_kernel(pos, own, *refs):
    total = own[...]
    for part in refs[:-1]:
        total = total + part[...].astype(F32)
    refs[-1][...] = total.astype(BF)


def copy_kernel(pos, value, out):
    out[...] = value[...]


def column_kernel(pos, *refs):
    blocks, out = refs[:-1], refs[-1]
    n = blocks[0].shape[0]
    for k, block in enumerate(blocks):
        out[pos[2] ^ k, 0:n] = block[...]
        if n < out.shape[1]:
            out[pos[2] ^ k, n:] = jnp.zeros((out.shape[1] - n, out.shape[2]), out.dtype)


def w2_place_kernel(pos, mine, other, out):
    g, _, cin = mine.shape
    n = out.shape[0] // (2 * g)
    for k, col in enumerate((mine, other)):
        for i in range(g):
            out[pl.ds(pl.multiple_of(((pos[1] ^ k) * g + i) * n, n), n), :] = col[i, 0:n].astype(F32)


def w1_place_kernel(pos, blocks, out, grad_k, grad_bd, grad_b1, small):
    g = len(blocks) // 2
    half = blocks[0].shape[1]
    n = out.shape[0] // g
    m = small.shape[0] // g
    for i, block in enumerate(blocks):
        cut = pl.ds(pl.multiple_of((pos[1] ^ (i // g)) * half, half), half)
        at = pos[2] ^ (i % g)
        out[pl.ds(pl.multiple_of(at * n, n), n), cut] = block[0:n, :].astype(F32)
        small[pl.ds(pl.multiple_of(at * m, m), m), cut] = block[n:, :].astype(F32)
    grad_k[...] = small[0:25, :]
    grad_bd[...] = small[25:26, :]
    grad_b1[...] = small[26:27, :]


def last_kernel(pos, cot, kept, arrived, last, mine, other, *refs):
    blocks, (out, out_w2, out_w1, grad_k, grad_bd, grad_b1, small) = refs[:-7], refs[-7:]
    finish_kernel(pos, cot, kept, arrived, last, out)
    w2_place_kernel(pos, mine, other, out_w2)
    w1_place_kernel(pos, blocks, out_w1, grad_k, grad_bd, grad_b1, small)


def summed(own, sends):
    for k, send in enumerate(sends):
        own = own + hop(send, 2 * (k + 1), 0).astype(F32)
    return own.astype(BF)


def halved(chunks):
    other = 3 - FIRST
    arrived = hop(jnp.stack([chunks[FIRST], chunks[3]]), 2 * FIRST, 0).astype(F32)
    return chunks[0] + arrived[0], chunks[other] + arrived[1]


def shards(inputs, cotangent, expand_w, expand_b, depth_k, depth_b, project_w):
    chan, dp = lax.axis_index("chan"), lax.axis_index("dp")
    pair, zpos = dp & 1, dp >> 1
    groups = lax.axis_size("dp") // 2
    own_rows, ncols, cin = inputs.shape
    nrows = 8 * own_rows
    hslice = expand_w.shape[1]
    half = hslice // 2
    npix = nrows * ncols
    pos = jnp.stack([pair * 4 + chan, pair, zpos, chan & 1]).astype(jnp.int32)

    full = array(nrows, ncols, half)
    mm = vpu = dict(flops=1024, nbytes=1024)
    long = dict(flops=2 * 10**10, nbytes=10**8)
    padded = array(half // LANES, nrows + 4, ncols + 2 * EDGE, LANES, dtype=F32)

    mine = array(*inputs.shape)
    w1, b1, taps, bd, w2, rows_own, cot_own, hidden, grad_pre = kernel(
        prepare_kernel, "prepare",
        (array(cin, half), array(1, half, dtype=F32), array(25, half, dtype=F32), array(1, half, dtype=F32),
         array(half, cin), mine, mine, padded, padded),
        (pos, expand_w, expand_b.reshape(1, hslice), depth_k, depth_b.reshape(1, hslice), project_w, inputs, cotangent),
    )

    def expand(order, into=(), after=(), edges=()):
        return kernel(
            lambda *refs: expand_kernel(order, *refs), "expand%d" % order[0], (padded, full) + edges,
            (pos, w1, b1, *(in_pieces[k] for k in order)), [pltpu.VMEM((own_rows, ncols, half), F32)],
            into=into, after=after, **mm,
        )

    in_pieces = {0: rows_own, 1: hop(inputs, 0, 1)}
    cot_core = hop(cotangent, 0, 1)
    steps = {4: (1, 0), 2: (0, 2), 6: (1, 2)}
    for k, step in steps.items():
        in_pieces[k] = hop(inputs, *step)
    first = expand((0, 1), (hidden,), after=(cot_core,))
    for k in (4, 2):
        in_pieces[k + 1] = hop(tied(in_pieces[k], first[0]), 0, 1)
    second = expand((2, 4), first)
    in_pieces[7] = hop(tied(in_pieces[6], second[1]), 0, 1)
    cot_pair = cross(tied(jnp.stack([cot_own, cot_core]), in_pieces[2], in_pieces[4]), 0)
    cot_far = hop(tied(cotangent, in_pieces[6], second[1]), *steps[6])
    in_pieces = [in_pieces[k] for k in range(8)]
    edges = (array(2, ncols, half),) * 2
    hidden, slope_one, *sent = expand((7,), expand((6, 3, 5), second), edges=edges)
    hid_near, hid_far = meet(sent[0], FLIP_HID), meet(sent[1], 1 - FLIP_HID)

    f32_full = array(nrows, ncols, half, dtype=F32)
    inner = kernel(
        lambda *refs: middle_kernel(True, *refs), "inner", (full, f32_full), (pos, taps, bd, hidden), **long
    )
    mixed, slope_two, hidden = kernel(
        lambda *refs: middle_kernel(False, *refs), "outer", (full, f32_full, padded),
        (pos, taps, bd, hid_near, hid_far), into=(*inner, hidden), **vpu,
    )
    cot_swap = hop(tied(cot_pair, slope_one), 0, 1)
    cot_last = hop(tied(cot_far, mixed), 0, 1)
    cot_pieces = (cot_own, cot_core, cot_pair, cot_far, cot_swap, cot_last)

    def project(pieces, into=(), after=(), edges=()):
        return kernel(
            lambda *refs: project_kernel(pieces, *refs), "project%d" % pieces[0], (padded,) + edges,
            (pos, w2, slope_two, *(cot_pieces[i] for i in pieces)), into=into, after=after, **mm,
        )

    def chunk_outs(rows, width):
        return (array(rows, width, dtype=F32),) + (array(rows, width),) * (groups - 1)

    half_done = project((0, 1, 2, 3), (grad_pre,))
    w2_chunks = kernel(
        w2_kernel, "w2", chunk_outs(half // groups, cin), (pos, mixed, *cot_pieces),
        [pltpu.VMEM((half, cin), F32)], after=half_done, **mm,
    )
    grad_pre, *sent = project((4, 5), half_done, (w2_chunks[0],), edges)
    gp_near, gp_far = meet(sent[0], FLIP_GP), meet(sent[1], 1 - FLIP_GP)
    tail = 16 * groups
    small = kernel(taps_kernel, "taps", array(tail, half, dtype=F32), (pos, hidden, grad_pre), **vpu)
    four = groups == 4
    w2_halves = halved(w2_chunks) if four else w2_chunks[:1]
    _, grad_act, grad_b1 = kernel(
        back_kernel, "back", (padded, full, array(1, half, dtype=F32)), (pos, taps, gp_near, gp_far, slope_one),
        [pltpu.VMEM((8, LANES), F32)], after=(small, *w2_halves), into=(grad_pre,), **vpu,
    )
    if four:
        w2_sent = hop(tied(w2_halves[1], small).astype(BF), 2 * (3 - FIRST), 0).astype(F32)
        w2_chunk = (tied(w2_halves[0], grad_act) + w2_sent).astype(BF)
    else:
        w2_chunk = summed(tied(w2_chunks[0], grad_act), w2_chunks[1:])
    w2_two = jnp.stack([w2_chunk, hop(w2_chunk, 4, 0)]) if four else None

    block = (own_rows, ncols, cin)
    two = (2, *block)
    to_core = kernel(core_kernel, "core", array(4, *block), (pos, grad_act, w1), after=(w2_chunk,), **mm)
    from_core = hop(to_core, 0, 1)
    w1_own, *w1_sends = kernel(
        w1_kernel, "w1", chunk_outs((cin + tail) // groups, half), (pos, grad_act, small, grad_b1, *in_pieces),
        [pltpu.VMEM((cin + tail, half), F32)], after=(w2_chunk, to_core), **mm,
    )
    going = kernel(
        chip_send_kernel, "chip_send", array(*two), (pos, grad_act, w1, from_core), after=(w1_own,), **mm
    )
    if four:
        w2_far = hop(tied(w2_two, going), 2, 0)
        w2_blocks = [w2_two[0], w2_far[0], w2_two[1], w2_far[1]]
    else:
        w2_blocks = [hop(w2_chunk, 2 * k, 0) if k else w2_chunk for k in range(groups)]
    arrived = cross(going, 0)
    kept = kernel(chip_keep_kernel, "chip_keep", array(*two, dtype=F32), (pos, grad_act, w1, from_core), after=(going,), **mm)
    w1_parts = [hop(send, 2 * (k + 1), 0) for k, send in enumerate(w1_sends)]
    w1_chunk = kernel(sum_kernel, "sum", array(*w1_own.shape), (pos, w1_own, *w1_parts), after=(kept,), **long)
    w1_side = hop(w1_chunk, 1, 0)
    w1_near = [hop(w1_chunk, 2 * k, 0) if k else w1_chunk for k in range(groups)]
    w2_col = kernel(
        column_kernel, "column", array(groups, half // groups + ROOM, cin), (pos, *w2_blocks), after=(w1_chunk,), **mm
    )
    w2_other = hop(w2_col, 1, 0)
    forward = kernel(
        forward_kernel, "forward", array(*block), (pos, kept, arrived), after=(w1_side,), **mm
    )
    onward = cross(forward, 1)
    w1_side = kernel(copy_kernel, "side", array(*w1_side.shape), (pos, w1_side), after=(w1_near[-1],), **long)
    w1_blocks = w1_near + [hop(w1_side, 2 * k, 0) if k else w1_side for k in range(groups)]
    line = array(1, hslice, dtype=F32)
    input_grad, out_w2, out_w1, out_k, out_bd, out_b1 = kernel(
        last_kernel, "last",
        (array(*block), array(hslice, cin, dtype=F32), array(cin, hslice, dtype=F32), array(25, hslice, dtype=F32), line, line),
        (pos, cot_own, kept, arrived, onward, w2_col, w2_other, *w1_blocks),
        [pltpu.VMEM((tail, hslice), F32)],
    )
    return (input_grad, out_w1, out_b1.reshape(hslice), out_k, out_bd.reshape(hslice), out_w2)


def solution(mesh):
    in_specs = (
        P(("dp", "chan"), None, None),
        P(("dp", "chan"), None, None),
        P(None, "chan"),
        P("chan"),
        P(None, "chan"),
        P("chan"),
        P("chan", None),
    )
    out_specs = (
        P(("dp", "chan"), None, None),
        P(None, "chan"),
        P("chan"),
        P(None, "chan"),
        P("chan"),
        P("chan", None),
    )
    return jax.shard_map(shards, mesh=mesh, in_specs=in_specs, out_specs=out_specs, check_vma=False)
```

```python
import jax
import jax.numpy as jnp
from jax import lax
from jax.experimental import pallas as pl
from jax.experimental.pallas import tpu as pltpu
from jax.sharding import PartitionSpec as P

BF = jnp.bfloat16
F32 = jnp.float32
AXES = ("dp", "chan")
VMEM = pl.BlockSpec(memory_space=pltpu.VMEM)
SMEM = pl.BlockSpec(memory_space=pltpu.SMEM)
ANY = pl.BlockSpec(memory_space=pl.ANY)
EDGE = 8
LANES = 128
FLIP_HID, FLIP_GP = 0, 1
FIRST = 2
ROOM = 0


def array(*shape, dtype=BF):
    return jax.ShapeDtypeStruct(shape, dtype)


def kernel(body, name, out, args, scratch=(), flops=0, nbytes=0, after=(), into=()):
    first, last = len(args), len(args) + len(after) + len(into)

    def run(*refs):
        body(*refs[:first], *refs[last:])

    return pl.pallas_call(
        run,
        out_shape=out,
        in_specs=[SMEM] + [VMEM] * (len(args) - 1) + [ANY] * len(after) + [VMEM] * len(into),
        out_specs=jax.tree.map(lambda _: VMEM, out),
        scratch_shapes=list(scratch),
        compiler_params=pltpu.CompilerParams(vmem_limit_bytes=16 * 1024 * 1024),
        cost_estimate=pl.CostEstimate(flops=flops, bytes_accessed=nbytes, transcendentals=0),
        input_output_aliases={len(args) + len(after) + i: i for i in range(len(into))},
        name=name,
    )(*args, *after, *into)


def gelu_parts(pre):
    cdf = 0.5 * (1.0 + lax.erf(pre * 0.7071067811865476))
    dens = jnp.exp(-0.5 * pre * pre) * 0.3989422804014327
    return pre * cdf, cdf + pre * dens


def hop(value, dp_xor, chan_xor):
    ndp, nchan = lax.axis_size("dp"), lax.axis_size("chan")
    pairs = [
        (d * nchan + c, (d ^ dp_xor) * nchan + (c ^ chan_xor))
        for d in range(ndp)
        for c in range(nchan)
    ]
    return lax.ppermute(value, AXES, pairs)


def cross(value, turn):
    ndp, nchan = lax.axis_size("dp"), lax.axis_size("chan")
    pairs = []
    for d in range(ndp):
        for c in range(nchan):
            to = (d ^ 1, c) if (c & 1) == turn else (d, c ^ 2)
            pairs.append((d * nchan + c, to[0] * nchan + to[1]))
    return lax.ppermute(value, AXES, pairs)


def meet(value, odd):
    ndp, nchan = lax.axis_size("dp"), lax.axis_size("chan")
    pairs = []
    for d in range(ndp):
        to = d + 2 if (d // 2) % 2 == odd else d - 2
        if 0 <= to < ndp:
            pairs += [(d * nchan + c, to * nchan + c) for c in range(nchan)]
    return lax.ppermute(value, AXES, pairs)


def tied(value, *others):
    return lax.optimization_barrier((value, *others))[0]


def prepare_kernel(pos, w1, b1, taps, b2, w2, rows, cot, w1_own, b1_own, taps_own, b2_own, w2_own, rows_own, cot_own, *pads):
    half = b1_own.shape[1]
    cut = pl.ds(pl.multiple_of(pos[1] * half, half), half)
    w1_own[...] = w1[:, cut]
    b1_own[...] = b1[:, cut]
    taps_own[...] = taps[:, cut]
    b2_own[...] = b2[:, cut]
    w2_own[...] = w2[cut, :]
    rows_own[...] = rows[...]
    cot_own[...] = cot[...]
    for pad in pads:
        zeros = jnp.zeros((pad.shape[0], pad.shape[1], EDGE, LANES), F32)
        pad[:, :, 0:EDGE, :] = zeros
        pad[:, :, pad.shape[2] - EDGE :, :] = zeros


def cuts(half):
    return [(c, slice(c * LANES, (c + 1) * LANES)) for c in range(half // LANES)]


def put_rows(pad, at, value):
    rows, ncols, half = value.shape
    value = value.astype(BF).astype(F32)
    for c, cut in cuts(half):
        pad[c, pl.ds(at + 2, rows), EDGE : EDGE + ncols, :] = value[:, :, cut]


def put_edges(pos, pad, edges, flip):
    _, ncols, half = edges[0].shape
    last = pad.shape[1] - 6
    odd = (pos[2] & 1) ^ flip
    for edge, at in zip(edges, (last * (1 - odd), last * odd)):
        for c, cut in cuts(half):
            edge[:, :, cut] = pad[c, pl.ds(at + 2, 2), EDGE : EDGE + ncols, :].astype(BF)


def put_halo(pos, pad, near, far, flip):
    _, ncols, half = near.shape
    last = pad.shape[1] - 2
    odd = (pos[2] & 1) ^ flip
    for edge, at in zip((near, far), (last * (1 - odd), last * odd)):
        for c, cut in cuts(half):
            pad[c, pl.ds(at, 2), EDGE : EDGE + ncols, :] = edge[:, :, cut].astype(F32)


def expand_kernel(order, pos, w, b, *refs):
    pieces, (hid, slope, *edges, pre) = refs[: len(order)], refs[len(order) :]
    n, ncols, cin = pieces[0].shape
    half = slope.shape[2]
    for k, piece in zip(order, pieces):
        at = (pos[0] ^ k) * n
        pre[...] = (
            jnp.dot(piece[...].reshape(n * ncols, cin), w[...], preferred_element_type=F32) + b[...]
        ).reshape(n, ncols, half)

        def body(r, carry, at=at):
            h, s = gelu_parts(pre[pl.ds(r, 1)])
            put_rows(hid, at + r, h)
            slope[pl.ds(at + r, 1)] = s.astype(BF)
            return carry

        lax.fori_loop(0, n, body, 0)
    if edges:
        put_edges(pos, hid, edges, FLIP_HID)


def conv_tiles(pad, taps, cut, ncols, starts, nr, cols, flip, emit):
    def body(i, carry):
        w0 = i * cols
        for r0 in starts:
            acc = [None] * nr
            for j in range(5):
                xs = [pad[r0 + q, pl.ds(w0 + (EDGE - 2) + j, cols), :] for q in range(nr + 4)]
                for q in range(5):
                    t = 5 * q + j
                    t = 24 - t if flip else t
                    for r in range(nr):
                        term = taps[t : t + 1, cut] * xs[r + q]
                        acc[r] = term if acc[r] is None else acc[r] + term
            emit(r0, pl.ds(pl.multiple_of(w0, cols), cols), acc)
        return carry

    lax.fori_loop(0, ncols // cols, body, 0)


def middle_kernel(inner, pos, taps, bias, *refs):
    if inner:
        pad, mixed, slope = refs
    else:
        near, far, mixed, slope, pad = refs
        put_halo(pos, pad, near, far, FLIP_HID)
    nrows, ncols, half = mixed.shape
    for c, cut in cuts(half):
        add = bias[:, cut]

        def emit(r0, w, acc, cut=cut, add=add):
            for r in range(len(acc)):
                m, s = gelu_parts(acc[r] + add)
                mixed[r0 + r, w, cut] = m.astype(BF)
                slope[r0 + r, w, cut] = s

        if inner:
            conv_tiles(pad.at[c], taps, cut, ncols, range(2, nrows - 2, 4), 4, 16, False, emit)
        else:
            conv_tiles(pad.at[c], taps, cut, ncols, (0, nrows - 2), 2, 32, False, emit)


def cot_blocks(pos, which, refs):
    core = pos[3]
    found = []
    for i, ref in zip(which, refs):
        if i in (2, 4):
            found += [((4 - 2 * core if i == 2 else 3 + 2 * core) + (j if i == 2 else -j), ref.at[j]) for j in range(2)]
        else:
            found.append(({0: 0, 1: 1, 3: 6, 5: 7}[i], ref))
    return found


def project_kernel(which, pos, weights, slope, *refs):
    pieces, (gp, *edges) = cot_blocks(pos, which, refs[: len(which)]), refs[len(which) :]
    n, ncols, cin = pieces[0][1].shape
    half = slope.shape[2]
    for k, piece in pieces:
        at = (pos[0] ^ k) * n
        res = lax.dot_general(
            piece[...].reshape(n * ncols, cin), weights[...], (((1,), (1,)), ((), ())), preferred_element_type=F32
        )
        put_rows(gp, at, res.reshape(n, ncols, half) * slope[pl.ds(at, n)])
    if edges:
        put_edges(pos, gp, edges, FLIP_GP)


def outer_sum(pos, total, pieces, values, swap):
    n, ncols, _ = pieces[0][1].shape
    for i, (k, piece) in enumerate(pieces):
        a = piece[...].reshape(n * ncols, -1)
        b = values[pl.ds((pos[0] ^ k) * n, n)].reshape(n * ncols, -1)
        if swap:
            a, b = b, a
        part = lax.dot_general(a, b, (((0,), (0,)), ((), ())), preferred_element_type=F32)
        if i == 0:
            total[0 : part.shape[0], :] = part
        else:
            total[0 : part.shape[0], :] += part


def w2_kernel(pos, mixed, *refs):
    pieces, outs, total = cot_blocks(pos, range(6), refs[:6]), refs[6:-1], refs[-1]
    outer_sum(pos, total, pieces, mixed, True)
    n = outs[0].shape[0]
    for k, ref in enumerate(outs):
        ref[...] = total[pl.ds(pl.multiple_of((pos[2] ^ k) * n, n), n), :].astype(ref.dtype)


def taps_kernel(pos, hid, gp, small):
    _, nrows, ncols, _ = hid.shape
    nrows, ncols = nrows - 4, ncols - 2 * EDGE
    small[...] = jnp.zeros_like(small)
    for c, cut in cuts(small.shape[1]):

        def body(i, accs, c=c):
            accs = list(accs)
            w0 = i * 8
            for j in range(5):
                xs = [hid[c, q, pl.ds(w0 + (EDGE - 2) + j, 8), :] for q in range(4)]
                for r in range(nrows):
                    xs.append(hid[c, r + 4, pl.ds(w0 + (EDGE - 2) + j, 8), :])
                    g = gp[c, r + 2, pl.ds(pl.multiple_of(w0 + EDGE, 8), 8), :]
                    for q in range(5):
                        accs[5 * q + j] = accs[5 * q + j] + xs[r + q] * g
                    if j == 0:
                        accs[25] = accs[25] + g
            return tuple(accs)

        zero = jnp.zeros((8, LANES), F32)
        accs = lax.fori_loop(0, ncols // 8, body, (zero,) * 26)
        for t in range(26):
            small[t : t + 1, cut] = jnp.sum(accs[t], axis=0, keepdims=True)


def back_kernel(pos, taps, near, far, slope, pad, act, grad_b, total):
    nrows, ncols, half = act.shape
    put_halo(pos, pad, near, far, FLIP_GP)
    for c, cut in cuts(half):
        total[...] = jnp.zeros_like(total)

        def emit(r0, w, acc, cut=cut):
            part = jnp.zeros((8, LANES), F32)
            for r in range(4):
                a = (acc[r] * slope[r0 + r, w, cut].astype(F32)).astype(BF)
                act[r0 + r, w, cut] = a
                part = part + jnp.sum(a.astype(F32).reshape(-1, 8, LANES), axis=0)
            total[...] += part

        conv_tiles(pad.at[c], taps, cut, ncols, range(0, nrows, 4), 4, 16, True, emit)
        grad_b[:, cut] = jnp.sum(total[...], axis=0, keepdims=True)


def w1_kernel(pos, act, small, grad_b, *refs):
    pieces, outs, total = refs[:8], refs[8:-1], refs[-1]
    outer_sum(pos, total, list(enumerate(pieces)), act, False)
    cin = pieces[0].shape[2]
    total[cin:, :] = small[...]
    total[cin + 26 : cin + 27, :] = grad_b[...]
    chunks = len(outs)
    n, m = cin // chunks, small.shape[0] // chunks
    for k, ref in enumerate(outs):
        at = pos[2] ^ k
        ref[0:n, :] = total[pl.ds(pl.multiple_of(at * n, n), n), :].astype(ref.dtype)
        ref[n:, :] = total[pl.ds(pl.multiple_of(cin + at * m, m), m), :].astype(ref.dtype)


def back_core_kernel(pos, taps, near, far, slope, w, pad, act, grad_b, to_core, total):
    back_kernel(pos, taps, near, far, slope, pad, act, grad_b, total)
    core_kernel(pos, act, w, to_core)


def share(pos, act, w, chip_xor, core):
    ncols, half = act.shape[1:]
    n = act.shape[0] // 8
    at = (((pos[0] // 2) ^ chip_xor) * 2 + core) * n
    return lax.dot_general(
        act[pl.ds(at, n)].reshape(n * ncols, half), w[...], (((1,), (1,)), ((), ())), preferred_element_type=F32
    ).reshape(n, ncols, -1)


def core_kernel(pos, act, w, out):
    for k in range(4):
        out[k] = share(pos, act, w, k, 1 - pos[3]).astype(BF)


def chip_send_kernel(pos, act, w, other, out):
    for i, k in enumerate((1 + pos[3], 3)):
        out[i] = (share(pos, act, w, k, pos[3]) + other[k].astype(F32)).astype(BF)


def chip_keep_kernel(pos, act, w, other, out):
    for i, k in enumerate((0, 2 - pos[3])):
        out[i] = share(pos, act, w, k, pos[3]) + other[k].astype(F32)


def forward_kernel(pos, kept, arrived, out):
    out[...] = (kept[1] + arrived[1].astype(F32)).astype(BF)


def finish_kernel(pos, cot, kept, arrived, last, out):
    out[...] = (cot[...].astype(F32) + (kept[0] + arrived[0].astype(F32) + last[...].astype(F32))).astype(BF)


def sum_kernel(pos, own, *refs):
    total = own[...]
    for part in refs[:-1]:
        total = total + part[...].astype(F32)
    refs[-1][...] = total.astype(BF)


def copy_kernel(pos, value, out):
    out[...] = value[...]


def column_kernel(pos, *refs):
    blocks, out = refs[:-1], refs[-1]
    n = blocks[0].shape[0]
    for k, block in enumerate(blocks):
        out[pos[2] ^ k, 0:n] = block[...]
        if n < out.shape[1]:
            out[pos[2] ^ k, n:] = jnp.zeros((out.shape[1] - n, out.shape[2]), out.dtype)


def w2_place_kernel(pos, mine, other, out):
    g, _, cin = mine.shape
    n = out.shape[0] // (2 * g)
    for k, col in enumerate((mine, other)):
        for i in range(g):
            out[pl.ds(pl.multiple_of(((pos[1] ^ k) * g + i) * n, n), n), :] = col[i, 0:n].astype(F32)


def w1_place_kernel(pos, blocks, out, grad_k, grad_bd, grad_b1, small):
    g = len(blocks) // 2
    half = blocks[0].shape[1]
    n = out.shape[0] // g
    m = small.shape[0] // g
    for i, block in enumerate(blocks):
        cut = pl.ds(pl.multiple_of((pos[1] ^ (i // g)) * half, half), half)
        at = pos[2] ^ (i % g)
        out[pl.ds(pl.multiple_of(at * n, n), n), cut] = block[0:n, :].astype(F32)
        small[pl.ds(pl.multiple_of(at * m, m), m), cut] = block[n:, :].astype(F32)
    grad_k[...] = small[0:25, :]
    grad_bd[...] = small[25:26, :]
    grad_b1[...] = small[26:27, :]


def last_kernel(pos, cot, kept, arrived, last, mine, other, *refs):
    blocks, (out, out_w2, out_w1, grad_k, grad_bd, grad_b1, small) = refs[:-7], refs[-7:]
    finish_kernel(pos, cot, kept, arrived, last, out)
    w2_place_kernel(pos, mine, other, out_w2)
    w1_place_kernel(pos, blocks, out_w1, grad_k, grad_bd, grad_b1, small)


def summed(own, sends):
    for k, send in enumerate(sends):
        own = own + hop(send, 2 * (k + 1), 0).astype(F32)
    return own.astype(BF)


def halved(chunks):
    other = 3 - FIRST
    arrived = hop(jnp.stack([chunks[FIRST], chunks[3]]), 2 * FIRST, 0).astype(F32)
    return chunks[0] + arrived[0], chunks[other] + arrived[1]


def shards(inputs, cotangent, expand_w, expand_b, depth_k, depth_b, project_w):
    chan, dp = lax.axis_index("chan"), lax.axis_index("dp")
    pair, zpos = dp & 1, dp >> 1
    groups = lax.axis_size("dp") // 2
    own_rows, ncols, cin = inputs.shape
    nrows = 8 * own_rows
    hslice = expand_w.shape[1]
    half = hslice // 2
    npix = nrows * ncols
    pos = jnp.stack([pair * 4 + chan, pair, zpos, chan & 1]).astype(jnp.int32)

    full = array(nrows, ncols, half)
    mm = vpu = dict(flops=1024, nbytes=1024)
    long = dict(flops=2 * 10**10, nbytes=10**8)
    padded = array(half // LANES, nrows + 4, ncols + 2 * EDGE, LANES, dtype=F32)

    mine = array(*inputs.shape)
    w1, b1, taps, bd, w2, rows_own, cot_own, hidden, grad_pre = kernel(
        prepare_kernel, "prepare",
        (array(cin, half), array(1, half, dtype=F32), array(25, half, dtype=F32), array(1, half, dtype=F32),
         array(half, cin), mine, mine, padded, padded),
        (pos, expand_w, expand_b.reshape(1, hslice), depth_k, depth_b.reshape(1, hslice), project_w, inputs, cotangent),
    )

    def expand(order, into=(), after=(), edges=()):
        return kernel(
            lambda *refs: expand_kernel(order, *refs), "expand%d" % order[0], (padded, full) + edges,
            (pos, w1, b1, *(in_pieces[k] for k in order)), [pltpu.VMEM((own_rows, ncols, half), F32)],
            into=into, after=after, **mm,
        )

    in_pieces = {0: rows_own, 1: hop(inputs, 0, 1)}
    cot_core = hop(cotangent, 0, 1)
    steps = {4: (1, 0), 2: (0, 2), 6: (1, 2)}
    for k, step in steps.items():
        in_pieces[k] = hop(inputs, *step)
    first = expand((0, 1), (hidden,), after=(cot_core,))
    for k in (4, 2):
        in_pieces[k + 1] = hop(tied(in_pieces[k], first[0]), 0, 1)
    second = expand((2, 4), first)
    in_pieces[7] = hop(tied(in_pieces[6], second[1]), 0, 1)
    cot_pair = cross(tied(jnp.stack([cot_own, cot_core]), in_pieces[2], in_pieces[4]), 0)
    cot_far = hop(tied(cotangent, in_pieces[6], second[1]), *steps[6])
    in_pieces = [in_pieces[k] for k in range(8)]
    edges = (array(2, ncols, half),) * 2
    hidden, slope_one, *sent = expand((7,), expand((6, 3, 5), second), edges=edges)
    hid_near, hid_far = meet(sent[0], FLIP_HID), meet(sent[1], 1 - FLIP_HID)

    f32_full = array(nrows, ncols, half, dtype=F32)
    inner = kernel(
        lambda *refs: middle_kernel(True, *refs), "inner", (full, f32_full), (pos, taps, bd, hidden), **long
    )
    mixed, slope_two, hidden = kernel(
        lambda *refs: middle_kernel(False, *refs), "outer", (full, f32_full, padded),
        (pos, taps, bd, hid_near, hid_far), into=(*inner, hidden), **vpu,
    )
    cot_swap = hop(tied(cot_pair, slope_one), 0, 1)
    cot_last = hop(tied(cot_far, mixed), 0, 1)
    cot_pieces = (cot_own, cot_core, cot_pair, cot_far, cot_swap, cot_last)

    def project(pieces, into=(), after=(), edges=()):
        return kernel(
            lambda *refs: project_kernel(pieces, *refs), "project%d" % pieces[0], (padded,) + edges,
            (pos, w2, slope_two, *(cot_pieces[i] for i in pieces)), into=into, after=after, **mm,
        )

    def chunk_outs(rows, width):
        return (array(rows, width, dtype=F32),) + (array(rows, width),) * (groups - 1)

    half_done = project((0, 1, 2, 3), (grad_pre,))
    w2_chunks = kernel(
        w2_kernel, "w2", chunk_outs(half // groups, cin), (pos, mixed, *cot_pieces),
        [pltpu.VMEM((half, cin), F32)], after=half_done, **mm,
    )
    grad_pre, *sent = project((4, 5), half_done, (w2_chunks[0],), edges)
    gp_near, gp_far = meet(sent[0], FLIP_GP), meet(sent[1], 1 - FLIP_GP)
    tail = 16 * groups
    small = kernel(taps_kernel, "taps", array(tail, half, dtype=F32), (pos, hidden, grad_pre), **vpu)
    four = groups == 4
    w2_halves = halved(w2_chunks) if four else w2_chunks[:1]
    block = (own_rows, ncols, cin)
    two = (2, *block)
    _, grad_act, grad_b1, to_core = kernel(
        back_core_kernel, "back", (padded, full, array(1, half, dtype=F32), array(4, *block)),
        (pos, taps, gp_near, gp_far, slope_one, w1), [pltpu.VMEM((8, LANES), F32)],
        after=(small, *w2_halves), into=(grad_pre,), **vpu,
    )
    from_core = hop(to_core, 0, 1)
    if four:
        w2_sent = hop(tied(w2_halves[1], small).astype(BF), 2 * (3 - FIRST), 0).astype(F32)
        w2_chunk = (tied(w2_halves[0], grad_act) + w2_sent).astype(BF)
    else:
        w2_chunk = summed(tied(w2_chunks[0], grad_act), w2_chunks[1:])
    w2_two = jnp.stack([w2_chunk, hop(w2_chunk, 4, 0)]) if four else None

    w1_own, *w1_sends = kernel(
        w1_kernel, "w1", chunk_outs((cin + tail) // groups, half), (pos, grad_act, small, grad_b1, *in_pieces),
        [pltpu.VMEM((cin + tail, half), F32)], after=(w2_chunk,), **long,
    )
    going = kernel(
        chip_send_kernel, "chip_send", array(*two), (pos, grad_act, w1, from_core), after=(w1_own,), **mm
    )
    if four:
        w2_far = hop(tied(w2_two, going), 2, 0)
        w2_blocks = [w2_two[0], w2_far[0], w2_two[1], w2_far[1]]
    else:
        w2_blocks = [hop(w2_chunk, 2 * k, 0) if k else w2_chunk for k in range(groups)]
    arrived = cross(going, 1)
    kept = kernel(chip_keep_kernel, "chip_keep", array(*two, dtype=F32), (pos, grad_act, w1, from_core), after=(going,), **mm)
    w1_parts = [hop(send, 2 * (k + 1), 0) for k, send in enumerate(w1_sends)]
    w1_chunk = kernel(sum_kernel, "sum", array(*w1_own.shape), (pos, w1_own, *w1_parts), after=(kept,), **long)
    w1_side = hop(w1_chunk, 1, 0)
    w1_near = [hop(w1_chunk, 2 * k, 0) if k else w1_chunk for k in range(groups)]
    w2_col = kernel(
        column_kernel, "column", array(groups, half // groups + ROOM, cin), (pos, *w2_blocks), after=(w1_chunk,), **mm
    )
    w2_other = hop(w2_col, 1, 0)
    forward = kernel(
        forward_kernel, "forward", array(*block), (pos, kept, arrived), after=(w1_side,), **mm
    )
    onward = cross(forward, 0)
    w1_side = kernel(copy_kernel, "side", array(*w1_side.shape), (pos, w1_side), after=(w1_near[-1],), **long)
    w1_blocks = w1_near + [hop(w1_side, 2 * k, 0) if k else w1_side for k in range(groups)]
    line = array(1, hslice, dtype=F32)
    input_grad, out_w2, out_w1, out_k, out_bd, out_b1 = kernel(
        last_kernel, "last",
        (array(*block), array(hslice, cin, dtype=F32), array(cin, hslice, dtype=F32), array(25, hslice, dtype=F32), line, line),
        (pos, cot_own, kept, arrived, onward, w2_col, w2_other, *w1_blocks),
        [pltpu.VMEM((tail, hslice), F32)],
    )
    return (input_grad, out_w1, out_b1.reshape(hslice), out_k, out_bd.reshape(hslice), out_w2)


def solution(mesh):
    in_specs = (
        P(("dp", "chan"), None, None),
        P(("dp", "chan"), None, None),
        P(None, "chan"),
        P("chan"),
        P(None, "chan"),
        P("chan"),
        P("chan", None),
    )
    out_specs = (
        P(("dp", "chan"), None, None),
        P(None, "chan"),
        P("chan"),
        P(None, "chan"),
        P("chan"),
        P("chan", None),
    )
    return jax.shard_map(shards, mesh=mesh, in_specs=in_specs, out_specs=out_specs, check_vma=False)
```

```python
import jax
import jax.numpy as jnp
from jax import lax
from jax.experimental import pallas as pl
from jax.experimental.pallas import tpu as pltpu
from jax.sharding import PartitionSpec as P

BF = jnp.bfloat16
F32 = jnp.float32
AXES = ("dp", "chan")
VMEM = pl.BlockSpec(memory_space=pltpu.VMEM)
SMEM = pl.BlockSpec(memory_space=pltpu.SMEM)
ANY = pl.BlockSpec(memory_space=pl.ANY)
EDGE = 8
LANES = 128
FLIP_HID, FLIP_GP = 0, 1
FIRST = 2
ROOM = 0


def array(*shape, dtype=BF):
    return jax.ShapeDtypeStruct(shape, dtype)


def kernel(body, name, out, args, scratch=(), flops=0, nbytes=0, after=(), into=()):
    first, last = len(args), len(args) + len(after) + len(into)

    def run(*refs):
        body(*refs[:first], *refs[last:])

    return pl.pallas_call(
        run,
        out_shape=out,
        in_specs=[SMEM] + [VMEM] * (len(args) - 1) + [ANY] * len(after) + [VMEM] * len(into),
        out_specs=jax.tree.map(lambda _: VMEM, out),
        scratch_shapes=list(scratch),
        compiler_params=pltpu.CompilerParams(vmem_limit_bytes=16 * 1024 * 1024),
        cost_estimate=pl.CostEstimate(flops=flops, bytes_accessed=nbytes, transcendentals=0),
        input_output_aliases={len(args) + len(after) + i: i for i in range(len(into))},
        name=name,
    )(*args, *after, *into)


def gelu_parts(pre):
    cdf = 0.5 * (1.0 + lax.erf(pre * 0.7071067811865476))
    dens = jnp.exp(-0.5 * pre * pre) * 0.3989422804014327
    return pre * cdf, cdf + pre * dens


def hop(value, dp_xor, chan_xor):
    ndp, nchan = lax.axis_size("dp"), lax.axis_size("chan")
    pairs = [
        (d * nchan + c, (d ^ dp_xor) * nchan + (c ^ chan_xor))
        for d in range(ndp)
        for c in range(nchan)
    ]
    return lax.ppermute(value, AXES, pairs)


def cross(value, turn):
    ndp, nchan = lax.axis_size("dp"), lax.axis_size("chan")
    pairs = []
    for d in range(ndp):
        for c in range(nchan):
            to = (d ^ 1, c) if (c & 1) == turn else (d, c ^ 2)
            pairs.append((d * nchan + c, to[0] * nchan + to[1]))
    return lax.ppermute(value, AXES, pairs)


def meet(value, odd):
    ndp, nchan = lax.axis_size("dp"), lax.axis_size("chan")
    pairs = []
    for d in range(ndp):
        to = d + 2 if (d // 2) % 2 == odd else d - 2
        if 0 <= to < ndp:
            pairs += [(d * nchan + c, to * nchan + c) for c in range(nchan)]
    return lax.ppermute(value, AXES, pairs)


def tied(value, *others):
    return lax.optimization_barrier((value, *others))[0]


def prepare_kernel(pos, w1, b1, taps, b2, w2, rows, cot, w1_own, b1_own, taps_own, b2_own, w2_own, rows_own, cot_own, *pads):
    half = b1_own.shape[1]
    cut = pl.ds(pl.multiple_of(pos[1] * half, half), half)
    w1_own[...] = w1[:, cut]
    b1_own[...] = b1[:, cut]
    taps_own[...] = taps[:, cut]
    b2_own[...] = b2[:, cut]
    w2_own[...] = w2[cut, :]
    rows_own[...] = rows[...]
    cot_own[...] = cot[...]
    for pad in pads:
        zeros = jnp.zeros((pad.shape[0], pad.shape[1], EDGE, LANES), F32)
        pad[:, :, 0:EDGE, :] = zeros
        pad[:, :, pad.shape[2] - EDGE :, :] = zeros


def cuts(half):
    return [(c, slice(c * LANES, (c + 1) * LANES)) for c in range(half // LANES)]


def put_rows(pad, at, value):
    rows, ncols, half = value.shape
    value = value.astype(BF).astype(F32)
    for c, cut in cuts(half):
        pad[c, pl.ds(at + 2, rows), EDGE : EDGE + ncols, :] = value[:, :, cut]


def put_edges(pos, pad, edges, flip):
    _, ncols, half = edges[0].shape
    last = pad.shape[1] - 6
    odd = (pos[2] & 1) ^ flip
    for edge, at in zip(edges, (last * (1 - odd), last * odd)):
        for c, cut in cuts(half):
            edge[:, :, cut] = pad[c, pl.ds(at + 2, 2), EDGE : EDGE + ncols, :].astype(BF)


def put_halo(pos, pad, near, far, flip):
    _, ncols, half = near.shape
    last = pad.shape[1] - 2
    odd = (pos[2] & 1) ^ flip
    for edge, at in zip((near, far), (last * (1 - odd), last * odd)):
        for c, cut in cuts(half):
            pad[c, pl.ds(at, 2), EDGE : EDGE + ncols, :] = edge[:, :, cut].astype(F32)


def expand_kernel(order, pos, w, b, *refs):
    pieces, (hid, slope, *edges, pre) = refs[: len(order)], refs[len(order) :]
    n, ncols, cin = pieces[0].shape
    half = slope.shape[2]
    for k, piece in zip(order, pieces):
        at = (pos[0] ^ k) * n
        pre[...] = (
            jnp.dot(piece[...].reshape(n * ncols, cin), w[...], preferred_element_type=F32) + b[...]
        ).reshape(n, ncols, half)

        def body(r, carry, at=at):
            h, s = gelu_parts(pre[pl.ds(r, 1)])
            put_rows(hid, at + r, h)
            slope[pl.ds(at + r, 1)] = s.astype(BF)
            return carry

        lax.fori_loop(0, n, body, 0)
    if edges:
        put_edges(pos, hid, edges, FLIP_HID)


def conv_tiles(pad, taps, cut, ncols, starts, nr, cols, flip, emit):
    def body(i, carry):
        w0 = i * cols
        for r0 in starts:
            acc = [None] * nr
            for j in range(5):
                xs = [pad[r0 + q, pl.ds(w0 + (EDGE - 2) + j, cols), :] for q in range(nr + 4)]
                for q in range(5):
                    t = 5 * q + j
                    t = 24 - t if flip else t
                    for r in range(nr):
                        term = taps[t : t + 1, cut] * xs[r + q]
                        acc[r] = term if acc[r] is None else acc[r] + term
            emit(r0, pl.ds(pl.multiple_of(w0, cols), cols), acc)
        return carry

    lax.fori_loop(0, ncols // cols, body, 0)


def middle_kernel(inner, pos, taps, bias, *refs):
    if inner:
        pad, mixed, slope = refs
    else:
        near, far, mixed, slope, pad = refs
        put_halo(pos, pad, near, far, FLIP_HID)
    nrows, ncols, half = mixed.shape
    for c, cut in cuts(half):
        add = bias[:, cut]

        def emit(r0, w, acc, cut=cut, add=add):
            for r in range(len(acc)):
                m, s = gelu_parts(acc[r] + add)
                mixed[r0 + r, w, cut] = m.astype(BF)
                slope[r0 + r, w, cut] = s

        if inner:
            conv_tiles(pad.at[c], taps, cut, ncols, range(2, nrows - 2, 4), 4, 16, False, emit)
        else:
            conv_tiles(pad.at[c], taps, cut, ncols, (0, nrows - 2), 2, 32, False, emit)


def cot_blocks(pos, which, refs):
    core = pos[3]
    found = []
    for i, ref in zip(which, refs):
        if i in (2, 4):
            found += [((4 - 2 * core if i == 2 else 3 + 2 * core) + (j if i == 2 else -j), ref.at[j]) for j in range(2)]
        else:
            found.append(({0: 0, 1: 1, 3: 6, 5: 7}[i], ref))
    return found


def project_kernel(which, pos, weights, slope, *refs):
    pieces, (gp, *edges) = cot_blocks(pos, which, refs[: len(which)]), refs[len(which) :]
    n, ncols, cin = pieces[0][1].shape
    half = slope.shape[2]
    for k, piece in pieces:
        at = (pos[0] ^ k) * n
        res = lax.dot_general(
            piece[...].reshape(n * ncols, cin), weights[...], (((1,), (1,)), ((), ())), preferred_element_type=F32
        )
        put_rows(gp, at, res.reshape(n, ncols, half) * slope[pl.ds(at, n)])
    if edges:
        put_edges(pos, gp, edges, FLIP_GP)


def outer_sum(pos, total, pieces, values, swap):
    n, ncols, _ = pieces[0][1].shape
    for i, (k, piece) in enumerate(pieces):
        a = piece[...].reshape(n * ncols, -1)
        b = values[pl.ds((pos[0] ^ k) * n, n)].reshape(n * ncols, -1)
        if swap:
            a, b = b, a
        part = lax.dot_general(a, b, (((0,), (0,)), ((), ())), preferred_element_type=F32)
        if i == 0:
            total[0 : part.shape[0], :] = part
        else:
            total[0 : part.shape[0], :] += part


def w2_kernel(pos, mixed, *refs):
    pieces, outs, total = cot_blocks(pos, range(6), refs[:6]), refs[6:-1], refs[-1]
    outer_sum(pos, total, pieces, mixed, True)
    n = outs[0].shape[0]
    for k, ref in enumerate(outs):
        ref[...] = total[pl.ds(pl.multiple_of((pos[2] ^ k) * n, n), n), :].astype(ref.dtype)


def products_kernel(pos, weights, slope, mixed, *refs):
    pieces, (gp, near, far, *outs) = refs[:6], refs[6:]
    project_kernel((4, 5), pos, weights, slope, *pieces[4:], gp, near, far)
    w2_kernel(pos, mixed, *pieces, *outs)


def taps_kernel(pos, hid, gp, small):
    _, nrows, ncols, _ = hid.shape
    nrows, ncols = nrows - 4, ncols - 2 * EDGE
    small[...] = jnp.zeros_like(small)
    for c, cut in cuts(small.shape[1]):

        def body(i, accs, c=c):
            accs = list(accs)
            w0 = i * 8
            for j in range(5):
                xs = [hid[c, q, pl.ds(w0 + (EDGE - 2) + j, 8), :] for q in range(4)]
                for r in range(nrows):
                    xs.append(hid[c, r + 4, pl.ds(w0 + (EDGE - 2) + j, 8), :])
                    g = gp[c, r + 2, pl.ds(pl.multiple_of(w0 + EDGE, 8), 8), :]
                    for q in range(5):
                        accs[5 * q + j] = accs[5 * q + j] + xs[r + q] * g
                    if j == 0:
                        accs[25] = accs[25] + g
            return tuple(accs)

        zero = jnp.zeros((8, LANES), F32)
        accs = lax.fori_loop(0, ncols // 8, body, (zero,) * 26)
        for t in range(26):
            small[t : t + 1, cut] = jnp.sum(accs[t], axis=0, keepdims=True)


def back_kernel(pos, taps, near, far, slope, pad, act, grad_b, total):
    nrows, ncols, half = act.shape
    put_halo(pos, pad, near, far, FLIP_GP)
    for c, cut in cuts(half):
        total[...] = jnp.zeros_like(total)

        def emit(r0, w, acc, cut=cut):
            part = jnp.zeros((8, LANES), F32)
            for r in range(4):
                a = (acc[r] * slope[r0 + r, w, cut].astype(F32)).astype(BF)
                act[r0 + r, w, cut] = a
                part = part + jnp.sum(a.astype(F32).reshape(-1, 8, LANES), axis=0)
            total[...] += part

        conv_tiles(pad.at[c], taps, cut, ncols, range(0, nrows, 4), 4, 16, True, emit)
        grad_b[:, cut] = jnp.sum(total[...], axis=0, keepdims=True)


def w1_kernel(pos, act, small, grad_b, *refs):
    pieces, outs, total = refs[:8], refs[8:-1], refs[-1]
    outer_sum(pos, total, list(enumerate(pieces)), act, False)
    cin = pieces[0].shape[2]
    total[cin:, :] = small[...]
    total[cin + 26 : cin + 27, :] = grad_b[...]
    chunks = len(outs)
    n, m = cin // chunks, small.shape[0] // chunks
    for k, ref in enumerate(outs):
        at = pos[2] ^ k
        ref[0:n, :] = total[pl.ds(pl.multiple_of(at * n, n), n), :].astype(ref.dtype)
        ref[n:, :] = total[pl.ds(pl.multiple_of(cin + at * m, m), m), :].astype(ref.dtype)


def back_core_kernel(pos, taps, near, far, slope, w, pad, act, grad_b, to_core, total):
    back_kernel(pos, taps, near, far, slope, pad, act, grad_b, total)
    core_kernel(pos, act, w, to_core)


def share(pos, act, w, chip_xor, core):
    ncols, half = act.shape[1:]
    n = act.shape[0] // 8
    at = (((pos[0] // 2) ^ chip_xor) * 2 + core) * n
    return lax.dot_general(
        act[pl.ds(at, n)].reshape(n * ncols, half), w[...], (((1,), (1,)), ((), ())), preferred_element_type=F32
    ).reshape(n, ncols, -1)


def core_kernel(pos, act, w, out):
    for k in range(4):
        out[k] = share(pos, act, w, k, 1 - pos[3]).astype(BF)


def chip_send_kernel(pos, act, w, other, out):
    for i, k in enumerate((1 + pos[3], 3)):
        out[i] = (share(pos, act, w, k, pos[3]) + other[k].astype(F32)).astype(BF)


def chip_keep_kernel(pos, act, w, other, out):
    for i, k in enumerate((0, 2 - pos[3])):
        out[i] = share(pos, act, w, k, pos[3]) + other[k].astype(F32)


def forward_kernel(pos, kept, arrived, out):
    out[...] = (kept[1] + arrived[1].astype(F32)).astype(BF)


def finish_kernel(pos, cot, kept, arrived, last, out):
    out[...] = (cot[...].astype(F32) + (kept[0] + arrived[0].astype(F32) + last[...].astype(F32))).astype(BF)


def sum_kernel(pos, own, *refs):
    total = own[...]
    for part in refs[:-1]:
        total = total + part[...].astype(F32)
    refs[-1][...] = total.astype(BF)


def copy_kernel(pos, value, out):
    out[...] = value[...]


def column_kernel(pos, *refs):
    blocks, out = refs[:-1], refs[-1]
    n = blocks[0].shape[0]
    for k, block in enumerate(blocks):
        out[pos[2] ^ k, 0:n] = block[...]
        if n < out.shape[1]:
            out[pos[2] ^ k, n:] = jnp.zeros((out.shape[1] - n, out.shape[2]), out.dtype)


def w2_place_kernel(pos, mine, other, out):
    g, _, cin = mine.shape
    n = out.shape[0] // (2 * g)
    for k, col in enumerate((mine, other)):
        for i in range(g):
            out[pl.ds(pl.multiple_of(((pos[1] ^ k) * g + i) * n, n), n), :] = col[i, 0:n].astype(F32)


def w1_place_kernel(pos, blocks, out, grad_k, grad_bd, grad_b1, small):
    g = len(blocks) // 2
    half = blocks[0].shape[1]
    n = out.shape[0] // g
    m = small.shape[0] // g
    for i, block in enumerate(blocks):
        cut = pl.ds(pl.multiple_of((pos[1] ^ (i // g)) * half, half), half)
        at = pos[2] ^ (i % g)
        out[pl.ds(pl.multiple_of(at * n, n), n), cut] = block[0:n, :].astype(F32)
        small[pl.ds(pl.multiple_of(at * m, m), m), cut] = block[n:, :].astype(F32)
    grad_k[...] = small[0:25, :]
    grad_bd[...] = small[25:26, :]
    grad_b1[...] = small[26:27, :]


def last_kernel(pos, cot, kept, arrived, last, mine, other, *refs):
    blocks, (out, out_w2, out_w1, grad_k, grad_bd, grad_b1, small) = refs[:-7], refs[-7:]
    finish_kernel(pos, cot, kept, arrived, last, out)
    w2_place_kernel(pos, mine, other, out_w2)
    w1_place_kernel(pos, blocks, out_w1, grad_k, grad_bd, grad_b1, small)


def summed(own, sends):
    for k, send in enumerate(sends):
        own = own + hop(send, 2 * (k + 1), 0).astype(F32)
    return own.astype(BF)


def halved(chunks):
    other = 3 - FIRST
    arrived = hop(jnp.stack([chunks[FIRST], chunks[3]]), 2 * FIRST, 0).astype(F32)
    return chunks[0] + arrived[0], chunks[other] + arrived[1]


def shards(inputs, cotangent, expand_w, expand_b, depth_k, depth_b, project_w):
    chan, dp = lax.axis_index("chan"), lax.axis_index("dp")
    pair, zpos = dp & 1, dp >> 1
    groups = lax.axis_size("dp") // 2
    own_rows, ncols, cin = inputs.shape
    nrows = 8 * own_rows
    hslice = expand_w.shape[1]
    half = hslice // 2
    npix = nrows * ncols
    pos = jnp.stack([pair * 4 + chan, pair, zpos, chan & 1]).astype(jnp.int32)

    full = array(nrows, ncols, half)
    mm = vpu = dict(flops=1024, nbytes=1024)
    long = dict(flops=2 * 10**10, nbytes=10**8)
    padded = array(half // LANES, nrows + 4, ncols + 2 * EDGE, LANES, dtype=F32)

    mine = array(*inputs.shape)
    w1, b1, taps, bd, w2, rows_own, cot_own, hidden, grad_pre = kernel(
        prepare_kernel, "prepare",
        (array(cin, half), array(1, half, dtype=F32), array(25, half, dtype=F32), array(1, half, dtype=F32),
         array(half, cin), mine, mine, padded, padded),
        (pos, expand_w, expand_b.reshape(1, hslice), depth_k, depth_b.reshape(1, hslice), project_w, inputs, cotangent),
    )

    def expand(order, into=(), after=(), edges=()):
        return kernel(
            lambda *refs: expand_kernel(order, *refs), "expand%d" % order[0], (padded, full) + edges,
            (pos, w1, b1, *(in_pieces[k] for k in order)), [pltpu.VMEM((own_rows, ncols, half), F32)],
            into=into, after=after, **mm,
        )

    in_pieces = {0: rows_own, 1: hop(inputs, 0, 1)}
    cot_core = hop(cotangent, 0, 1)
    steps = {4: (1, 0), 2: (0, 2), 6: (1, 2)}
    for k, step in steps.items():
        in_pieces[k] = hop(inputs, *step)
    first = expand((0, 1), (hidden,), after=(cot_core,))
    for k in (4, 2):
        in_pieces[k + 1] = hop(tied(in_pieces[k], first[0]), 0, 1)
    second = expand((2, 4), first)
    in_pieces[7] = hop(tied(in_pieces[6], second[1]), 0, 1)
    cot_pair = cross(tied(jnp.stack([cot_own, cot_core]), in_pieces[2], in_pieces[4]), 0)
    cot_far = hop(tied(cotangent, in_pieces[6], second[1]), *steps[6])
    in_pieces = [in_pieces[k] for k in range(8)]
    edges = (array(2, ncols, half),) * 2
    hidden, slope_one, *sent = expand((7,), expand((6, 3, 5), second), edges=edges)
    hid_near, hid_far = meet(sent[0], FLIP_HID), meet(sent[1], 1 - FLIP_HID)

    f32_full = array(nrows, ncols, half, dtype=F32)
    inner = kernel(
        lambda *refs: middle_kernel(True, *refs), "inner", (full, f32_full), (pos, taps, bd, hidden), **long
    )
    mixed, slope_two, hidden = kernel(
        lambda *refs: middle_kernel(False, *refs), "outer", (full, f32_full, padded),
        (pos, taps, bd, hid_near, hid_far), into=(*inner, hidden), **vpu,
    )
    cot_swap = hop(tied(cot_pair, slope_one), 0, 1)
    cot_last = hop(tied(cot_far, mixed), 0, 1)
    cot_pieces = (cot_own, cot_core, cot_pair, cot_far, cot_swap, cot_last)

    def project(pieces, into=(), after=(), edges=()):
        return kernel(
            lambda *refs: project_kernel(pieces, *refs), "project%d" % pieces[0], (padded,) + edges,
            (pos, w2, slope_two, *(cot_pieces[i] for i in pieces)), into=into, after=after, **mm,
        )

    def chunk_outs(rows, width):
        return (array(rows, width, dtype=F32),) + (array(rows, width),) * (groups - 1)

    half_done = project((0, 1, 2, 3), (grad_pre,))
    grad_pre, *rest = kernel(
        products_kernel, "products", (padded,) + edges + chunk_outs(half // groups, cin),
        (pos, w2, slope_two, mixed, *cot_pieces), [pltpu.VMEM((half, cin), F32)], into=half_done, **mm,
    )
    sent, w2_chunks = rest[:2], rest[2:]
    gp_near, gp_far = meet(sent[0], FLIP_GP), meet(sent[1], 1 - FLIP_GP)
    tail = 16 * groups
    small = kernel(taps_kernel, "taps", array(tail, half, dtype=F32), (pos, hidden, grad_pre), **vpu)
    four = groups == 4
    w2_halves = halved(w2_chunks) if four else w2_chunks[:1]
    block = (own_rows, ncols, cin)
    two = (2, *block)
    _, grad_act, grad_b1, to_core = kernel(
        back_core_kernel, "back", (padded, full, array(1, half, dtype=F32), array(4, *block)),
        (pos, taps, gp_near, gp_far, slope_one, w1), [pltpu.VMEM((8, LANES), F32)],
        after=(small, *w2_halves), into=(grad_pre,), **vpu,
    )
    from_core = hop(to_core, 0, 1)
    if four:
        w2_sent = hop(tied(w2_halves[1], small).astype(BF), 2 * (3 - FIRST), 0).astype(F32)
        w2_chunk = (tied(w2_halves[0], grad_act) + w2_sent).astype(BF)
    else:
        w2_chunk = summed(tied(w2_chunks[0], grad_act), w2_chunks[1:])
    w2_two = jnp.stack([w2_chunk, hop(w2_chunk, 4, 0)]) if four else None

    w1_own, *w1_sends = kernel(
        w1_kernel, "w1", chunk_outs((cin + tail) // groups, half), (pos, grad_act, small, grad_b1, *in_pieces),
        [pltpu.VMEM((cin + tail, half), F32)], after=(w2_chunk,), **long,
    )
    going = kernel(
        chip_send_kernel, "chip_send", array(*two), (pos, grad_act, w1, from_core), after=(w1_own,), **mm
    )
    if four:
        w2_far = hop(tied(w2_two, going), 2, 0)
        w2_blocks = [w2_two[0], w2_far[0], w2_two[1], w2_far[1]]
    else:
        w2_blocks = [hop(w2_chunk, 2 * k, 0) if k else w2_chunk for k in range(groups)]
    arrived = cross(going, 1)
    kept = kernel(chip_keep_kernel, "chip_keep", array(*two, dtype=F32), (pos, grad_act, w1, from_core), after=(going,), **mm)
    w1_parts = [hop(send, 2 * (k + 1), 0) for k, send in enumerate(w1_sends)]
    w1_chunk = kernel(sum_kernel, "sum", array(*w1_own.shape), (pos, w1_own, *w1_parts), after=(kept,), **long)
    w1_side = hop(w1_chunk, 1, 0)
    w1_near = [hop(w1_chunk, 2 * k, 0) if k else w1_chunk for k in range(groups)]
    w2_col = kernel(
        column_kernel, "column", array(groups, half // groups + ROOM, cin), (pos, *w2_blocks), after=(w1_chunk,), **mm
    )
    w2_other = hop(w2_col, 1, 0)
    forward = kernel(
        forward_kernel, "forward", array(*block), (pos, kept, arrived), after=(w1_side,), **mm
    )
    onward = cross(forward, 0)
    w1_side = kernel(copy_kernel, "side", array(*w1_side.shape), (pos, w1_side), after=(w1_near[-1],), **long)
    w1_blocks = w1_near + [hop(w1_side, 2 * k, 0) if k else w1_side for k in range(groups)]
    line = array(1, hslice, dtype=F32)
    input_grad, out_w2, out_w1, out_k, out_bd, out_b1 = kernel(
        last_kernel, "last",
        (array(*block), array(hslice, cin, dtype=F32), array(cin, hslice, dtype=F32), array(25, hslice, dtype=F32), line, line),
        (pos, cot_own, kept, arrived, onward, w2_col, w2_other, *w1_blocks),
        [pltpu.VMEM((tail, hslice), F32)],
    )
    return (input_grad, out_w1, out_b1.reshape(hslice), out_k, out_bd.reshape(hslice), out_w2)


def solution(mesh):
    in_specs = (
        P(("dp", "chan"), None, None),
        P(("dp", "chan"), None, None),
        P(None, "chan"),
        P("chan"),
        P(None, "chan"),
        P("chan"),
        P("chan", None),
    )
    out_specs = (
        P(("dp", "chan"), None, None),
        P(None, "chan"),
        P("chan"),
        P(None, "chan"),
        P("chan"),
        P("chan", None),
    )
    return jax.shard_map(shards, mesh=mesh, in_specs=in_specs, out_specs=out_specs, check_vma=False)
```
